32 devices in a mesh: groups: 2 (over y), markov: 4 (over z), storage: 2 (over x), sub: 2 (over core).
Axes of the slice: x: 2, y: 2, z: 4, core: 2. Of those that a mesh axis runs over, the one named last changes fastest.
Arguments:
- expected_cot: bfloat16 [8192, 2048], P(('groups', 'markov'), ('storage', 'sub')), parts along dimension 0, may hold values from -192 to 192
- value_next: bfloat16 [8192, 2048], P(('groups', 'markov'), ('storage', 'sub')), parts along dimension 0, may hold values from -0.0024414062 to 0.0024414062
- transition: bfloat16 [8192, 4096], P(('groups', 'storage', 'sub'), 'markov'), parts along dimension 0, may hold values from 6.1035156e-05 to 0.0009765625
- section: int32 [2], P('groups'), parts along dimension 0, may hold values from 0 to 51
Outputs:
- section_adjoint: float32 [8192, 2048], P(('groups', 'markov'), ('storage', 'sub')), parts along dimension 0
- transition_grad: float32 [8192, 4096], P(('groups', 'storage', 'sub'), 'markov'), parts along dimension 0
The draws below stay inside these ranges and needn't reach their ends.
There are 2 independent parts, one for each index of `groups`. The reference program is written for one: setup_inputs(seed, part) draws one part's arguments, and reference() takes and returns one part's arrays. A program takes and returns all parts, laid end to end along the dimension named above; each array names one. Nothing has to cross between parts.
All inputs are finite; a program needn't handle non-finite values.
Results may differ from the reference program's by a relative error of at most 0.0003.
Values may be sent and summed in bfloat16 or wider, within the bound.
No kernel may reach another device: no remote copies, remote signals or barrier semaphores. Data moves between devices by JAX's collectives and lax.ppermute only.
A program may use at most 64 MiB of HBM per device.

```python
import math
import jax
import jax.numpy as jnp
from jax import lax

M = 4096
SECTIONS = 52
CELLS = 2048


def steps_of(own_key, shape, shards, smallest, top_value):
    def one(dim, shards_of):
        heights = jax.random.uniform(jax.random.fold_in(jax.random.fold_in(own_key, 6), dim), (shards_of,), jnp.float32, smallest / len(shards), top_value / len(shards))
        return jnp.repeat(jnp.exp(heights), shape[dim] // shards_of).reshape((-1,) + (1,) * (len(shape) - dim - 1))

    loudness = one(*shards[0])
    for cut in shards[1:]:
        loudness = loudness * one(*cut)
    return loudness


def scatter_about(key, extent, width, reach, split=(), held_as=jnp.bfloat16):
    drawn = width * jax.random.normal(key, extent, jnp.float32)
    if split:
        drawn = drawn * steps_of(key, extent, split, -0.22, 0.18)
    return jnp.clip(drawn, -reach, reach).astype(held_as)


def setup_inputs(seed: int = 0, part: int = 0) -> dict:
    keys = jax.random.split(jax.random.key(seed), 5)
    own_keys = jax.random.split(jax.random.fold_in(keys[4], part), 5)
    expected_cot = scatter_about(own_keys[0], (M, CELLS), 32.0, 192.0, ((0, 4), (1, 4)))
    value_next = scatter_about(own_keys[1], (M, CELLS), 0.0004, 0.0024414062, ((0, 4), (1, 4)))
    transition = jnp.clip(jnp.exp(math.log(0.0009765625) - 2.7725887 * jax.random.uniform(own_keys[2], (M, M), jnp.float32) ** steps_of(own_keys[2], (M, M), ((0, 4), (1, 4)), -0.2, 0.2)), 6.103515625e-05, 0.0009765625).astype(jnp.bfloat16)
    section = jax.random.randint(own_keys[3], (1,), 0, SECTIONS).astype(jnp.int32)
    return {"expected_cot": expected_cot, "value_next": value_next, "transition": transition, "section": section}


discount_rate = 0.97


def reference(expected_cot, value_next, transition, section):
    discount_factor = jnp.exp(section[0].astype(jnp.float32) * jnp.log(jnp.float32(discount_rate)))
    adjoint_sum = lax.dot_general(transition, expected_cot, (((0,), (0,)), ((), ())), preferred_element_type=jnp.float32)
    gradient_sum = lax.dot_general(expected_cot, value_next, (((1,), (1,)), ((), ())), preferred_element_type=jnp.float32)
    return discount_factor * adjoint_sum, discount_factor * gradient_sum
```

```python
import jax
import jax.numpy as jnp
from jax import lax
from jax.sharding import PartitionSpec as P

discount_rate = 0.97
AXES = ("groups", "markov", "storage", "sub")


def factor_of(section):
    return jnp.exp(section[0].astype(jnp.float32) * jnp.log(jnp.float32(discount_rate)))


def plain_shards(expected_cot, value_next, transition, section):
    discount_factor = factor_of(section)
    cotangent_all = lax.all_gather(expected_cot, "markov", axis=0, tiled=True)
    adjoint_sum = lax.dot_general(
        lax.all_gather(transition, ("storage", "sub"), axis=0, tiled=True),
        cotangent_all,
        (((0,), (0,)), ((), ())),
        preferred_element_type=jnp.float32,
    )
    own_states = lax.all_to_all(
        cotangent_all, ("storage", "sub"), split_axis=0, concat_axis=1, tiled=True
    )
    gathered_values = lax.all_gather(value_next, ("storage", "sub"), axis=1, tiled=True)
    gradient_sum = lax.dot_general(
        own_states, gathered_values, (((1,), (1,)), ((), ())), preferred_element_type=jnp.float32
    )
    return (discount_factor * adjoint_sum, discount_factor * gradient_sum)


def tdot(a, b):
    return lax.dot_general(a, b, (((0,), (0,)), ((), ())), preferred_element_type=jnp.float32)


def dott(a, b):
    return lax.dot_general(a, b, (((1,), (1,)), ((), ())), preferred_element_type=jnp.float32)


def two_line_shards(sizes):
    groups, layers, sides, cores = sizes

    def index(g, z, s, c):
        return ((g * layers + z) * sides + s) * cores + c

    def level_moves(moves):
        at = lambda s, level: level if s == 0 else layers - 1 - level
        return [
            (index(g, at(s, a), s, c), index(g, at(s, b), s, c))
            for g in range(groups) for s in range(sides) for c in range(cores) for a, b in moves
        ]

    cross_pairs = [
        (index(g, z, s, c), index(g, z, 1 - s, c))
        for g in range(groups) for z in range(layers) for s in range(sides) for c in range(cores)
    ]
    core_pairs = [
        (index(g, z, s, c), index(g, z, s, 1 - c))
        for g in range(groups) for z in range(layers) for s in range(sides) for c in range(cores)
    ]

    def send(array, pairs):
        return lax.ppermute(array, AXES, pairs)

    def shards(expected_cot, value_next, transition, section):
        df = factor_of(section)
        z, s, c = lax.axis_index("markov"), lax.axis_index("storage"), lax.axis_index("sub")
        level = jnp.where(s == 0, z, layers - 1 - z)
        first = (c + s) % 2 == 0
        half = expected_cot.shape[1] // 2
        ep, eq = expected_cot[:, :half], expected_cot[:, half:]
        vp, vq = value_next[:, :half], value_next[:, half:]
        far = level >= 2

        def pick(l0, l1, l2, l3):
            return jnp.where(level < 2, jnp.where(level == 0, l0, l1), jnp.where(level == 2, l2, l3))

        up = lambda a, *levels: send(a, level_moves([(i, i + 1) for i in levels]))
        down = lambda a, *levels: send(a, level_moves([(i, i - 1) for i in levels]))
        cross = lambda a: send(a, cross_pairs)
        swap = lambda a: send(a, core_pairs)

        t_other = swap(transition)
        v_other = swap(value_next)
        x0 = cross(jnp.where(far, ep, vp))
        u0 = up(ep, 0, 1)
        d0 = down(eq, 3, 2)
        x1 = cross(jnp.where(far, eq, vq))
        u1 = up(jnp.where(level == 2, u0, x0), 0, 1, 2)
        d1 = down(d0, 2, 1)
        x2 = cross(jnp.where(far, vp, jnp.where(level == 1, d0, d1)))
        u2 = up(jnp.where(level == 0, x1, u1), 0, 1, 2)
        d2 = down(d1, 1)
        x3 = cross(jnp.where(far, vq, jnp.where(level == 1, d1, d2)))
        u3 = up(pick(eq, u0, u2, u2), 0, 1, 2)
        d3 = down(x0, 1)
        b0p, b1p = pick(x0, u1, u2, u3), pick(d3, x0, u1, u2)
        bp_own, bp_other = jnp.where(first, b0p, b1p), jnp.where(first, b1p, b0p)
        part_p = cross(tdot(transition, bp_own) + tdot(t_other, bp_other))
        u4 = up(jnp.where(level == 1, eq, u3), 1, 2)
        d4 = down(x1, 1)
        b0q, b1q = pick(x1, u2, x3, x3), pick(d4, x1, x2, x2)
        bq_own, bq_other = jnp.where(first, b0q, b1q), jnp.where(first, b1q, b0q)
        part_q = cross(tdot(transition, bq_own) + tdot(t_other, bq_other))
        u5 = up(jnp.where(level == 1, u3, u4), 1, 2)
        d5 = down(expected_cot, 1)
        u6 = up(u5, 2)

        vfar = jnp.concatenate([jnp.where(far, x0, x2), jnp.where(far, x1, x3)], 1)
        vfar_other = swap(vfar)
        bp_swapped, bq_swapped = swap(bp_other), swap(bq_other)
        b_all = jnp.concatenate([bp_own, bq_own, bp_swapped, bq_swapped], 1)
        grad = dott(b_all, jnp.concatenate([vfar, vfar_other], 1))

        a0p, a1p = pick(ep, u0, u3, u4), pick(d5[:, :half], ep, u0, u1)
        ap_own, ap_other = jnp.where(first, a0p, a1p), jnp.where(first, a1p, a0p)
        a0q, a1q = pick(eq, u3, u5, u6), pick(d5[:, half:], eq, u4, u5)
        aq_own, aq_other = jnp.where(first, a0q, a1q), jnp.where(first, a1q, a0q)
        a_own = jnp.concatenate([ap_own, aq_own], 1)
        a_other = jnp.concatenate([ap_other, aq_other], 1)
        a_swapped = jnp.concatenate([swap(ap_other), swap(aq_other)], 1)
        grad = grad + dott(
            jnp.concatenate([a_own, a_swapped], 1), jnp.concatenate([value_next, v_other], 1)
        )
        adjoint = tdot(transition, a_own) + tdot(t_other, a_other)
        adjoint = adjoint + jnp.concatenate([part_p, part_q], 1)
        return df * adjoint, df * grad

    return shards


def solution(mesh):
    sizes = tuple(mesh.shape[a] for a in AXES)
    shards = two_line_shards(sizes) if sizes[1:] == (4, 2, 2) else plain_shards
    return jax.shard_map(
        shards,
        mesh=mesh,
        in_specs=(
            P(("groups", "markov"), ("storage", "sub")),
            P(("groups", "markov"), ("storage", "sub")),
            P(("groups", "storage", "sub"), "markov"),
            P("groups"),
        ),
        out_specs=(
            P(("groups", "markov"), ("storage", "sub")),
            P(("groups", "storage", "sub"), "markov"),
        ),
        check_vma=False,
    )
```

```python
import jax
import jax.numpy as jnp
from jax import lax
from jax.sharding import PartitionSpec as P

discount_rate = 0.97
AXES = ("groups", "markov", "storage", "sub")


def factor_of(section):
    return jnp.exp(section[0].astype(jnp.float32) * jnp.log(jnp.float32(discount_rate)))


def plain_shards(expected_cot, value_next, transition, section):
    discount_factor = factor_of(section)
    cotangent_all = lax.all_gather(expected_cot, "markov", axis=0, tiled=True)
    adjoint_sum = lax.dot_general(
        lax.all_gather(transition, ("storage", "sub"), axis=0, tiled=True),
        cotangent_all,
        (((0,), (0,)), ((), ())),
        preferred_element_type=jnp.float32,
    )
    own_states = lax.all_to_all(
        cotangent_all, ("storage", "sub"), split_axis=0, concat_axis=1, tiled=True
    )
    gathered_values = lax.all_gather(value_next, ("storage", "sub"), axis=1, tiled=True)
    gradient_sum = lax.dot_general(
        own_states, gathered_values, (((1,), (1,)), ((), ())), preferred_element_type=jnp.float32
    )
    return (discount_factor * adjoint_sum, discount_factor * gradient_sum)


def tdot(a, b):
    return lax.dot_general(a, b, (((0,), (0,)), ((), ())), preferred_element_type=jnp.float32)


def dott(a, b):
    return lax.dot_general(a, b, (((1,), (1,)), ((), ())), preferred_element_type=jnp.float32)


def after(array, *others):
    return lax.optimization_barrier((array,) + others)[0]


def two_side_shards(sizes):
    groups, layers, sides, cores = sizes
    places = [(g, z, s, c) for g in range(groups) for z in range(layers) for s in range(sides) for c in range(cores)]
    index = {place: i for i, place in enumerate(places)}

    def pairs(move, chosen=lambda g, z, s, c: True):
        return [(index[p], index[move(*p)]) for p in places if chosen(*p)]

    def is_home(g, z, s, c):
        return z // 2 == s

    def is_away(g, z, s, c):
        return z // 2 != s

    def jumped(g, z, s, c):
        return (g, z ^ 2, s, c)

    cross_pairs = pairs(lambda g, z, s, c: (g, z, 1 - s, c))
    step_pairs = pairs(lambda g, z, s, c: (g, z ^ 1, s, c))
    core_pairs = pairs(lambda g, z, s, c: (g, z, s, 1 - c))
    home_jump_pairs, away_jump_pairs = pairs(jumped, is_home), pairs(jumped, is_away)

    def cross(a):
        return lax.ppermute(a, AXES, cross_pairs)

    def step(a):
        return lax.ppermute(a, AXES, step_pairs)

    def swap(a):
        return lax.ppermute(a, AXES, core_pairs)

    def home_jump(a):
        return lax.ppermute(a, AXES, home_jump_pairs)

    def away_jump(a):
        return lax.ppermute(a, AXES, away_jump_pairs)

    def shards(expected_cot, value_next, transition, section):
        df = factor_of(section)
        z, s, c = lax.axis_index("markov"), lax.axis_index("storage"), lax.axis_index("sub")
        home = z // 2 == s
        mine = z % 2 == c
        half = expected_cot.shape[1] // 2
        ep, eq = expected_cot[:, :half], expected_cot[:, half:]
        vp, vq = value_next[:, :half], value_next[:, half:]

        x1 = cross(jnp.where(home, vp, ep))
        jq = away_jump(eq)
        t_other = swap(transition)
        v_other = swap(value_next)
        t_near, t_next = jnp.where(mine, transition, t_other), jnp.where(mine, t_other, transition)

        def adjoint_of(near, far):
            return tdot(t_near, near) + tdot(t_next, far)

        def own_and_swapped(near, far):
            return jnp.where(mine, near, far), swap(jnp.where(mine, far, near))

        x2 = cross(after(jnp.where(home, vq, vp), x1))
        jp = home_jump(x1)
        x3 = cross(after(jnp.where(home, jq, vq), x2))
        jq2 = away_jump(x3)
        bp = jnp.where(home, x1, jp)
        bp_next = step(bp)
        jap = home_jump(after(ep, jp))
        part_p = cross(adjoint_of(bp, bp_next))
        bq = jnp.where(home, jq2, x3)
        bq_next = step(after(bq, bp_next))
        part_q = cross(adjoint_of(bq, bq_next))
        ap = jnp.where(home, ep, jap)
        ap_next = step(after(ap, bq_next))
        jaq = home_jump(after(eq, jap))
        aq = jnp.where(home, eq, jaq)
        aq_next = step(after(aq, ap_next))

        v_across = jnp.concatenate([jnp.where(home, x2, x1), jnp.where(home, x3, x2)], 1)
        v_across_other = swap(v_across)
        bp_own, bp_swapped = own_and_swapped(bp, bp_next)
        bq_own, bq_swapped = own_and_swapped(bq, bq_next)
        grad = dott(
            jnp.concatenate([bp_own, bq_own, bp_swapped, bq_swapped], 1),
            jnp.concatenate([v_across, v_across_other], 1),
        )
        ap_own, ap_swapped = own_and_swapped(ap, ap_next)
        aq_own, aq_swapped = own_and_swapped(aq, aq_next)
        grad = grad + dott(
            jnp.concatenate([ap_own, aq_own, ap_swapped, aq_swapped], 1),
            jnp.concatenate([value_next, v_other], 1),
        )
        adjoint = jnp.concatenate([adjoint_of(ap, ap_next) + part_p, adjoint_of(aq, aq_next) + part_q], 1)
        return df * adjoint, df * grad

    return shards


def solution(mesh):
    sizes = tuple(mesh.shape[a] for a in AXES)
    shards = two_side_shards(sizes) if sizes[1:] == (4, 2, 2) else plain_shards
    return jax.shard_map(
        shards,
        mesh=mesh,
        in_specs=(
            P(("groups", "markov"), ("storage", "sub")),
            P(("groups", "markov"), ("storage", "sub")),
            P(("groups", "storage", "sub"), "markov"),
            P("groups"),
        ),
        out_specs=(
            P(("groups", "markov"), ("storage", "sub")),
            P(("groups", "storage", "sub"), "markov"),
        ),
        check_vma=False,
    )
```

```python
import jax
import jax.numpy as jnp
from jax import lax
from jax.sharding import PartitionSpec as P

discount_rate = 0.97
AXES = ("groups", "markov", "storage", "sub")


def factor_of(section):
    return jnp.exp(section[0].astype(jnp.float32) * jnp.log(jnp.float32(discount_rate)))


def plain_shards(expected_cot, value_next, transition, section):
    discount_factor = factor_of(section)
    cotangent_all = lax.all_gather(expected_cot, "markov", axis=0, tiled=True)
    adjoint_sum = lax.dot_general(
        lax.all_gather(transition, ("storage", "sub"), axis=0, tiled=True),
        cotangent_all,
        (((0,), (0,)), ((), ())),
        preferred_element_type=jnp.float32,
    )
    own_states = lax.all_to_all(
        cotangent_all, ("storage", "sub"), split_axis=0, concat_axis=1, tiled=True
    )
    gathered_values = lax.all_gather(value_next, ("storage", "sub"), axis=1, tiled=True)
    gradient_sum = lax.dot_general(
        own_states, gathered_values, (((1,), (1,)), ((), ())), preferred_element_type=jnp.float32
    )
    return (discount_factor * adjoint_sum, discount_factor * gradient_sum)


def tdot(a, b):
    return lax.dot_general(a, b, (((0,), (0,)), ((), ())), preferred_element_type=jnp.float32)


def dott(a, b):
    return lax.dot_general(a, b, (((1,), (1,)), ((), ())), preferred_element_type=jnp.float32)


def after(array, *others):
    return lax.optimization_barrier((array,) + others)[0]


def two_side_shards(sizes):
    groups, layers, sides, cores = sizes
    places = [(g, z, s, c) for g in range(groups) for z in range(layers) for s in range(sides) for c in range(cores)]
    index = {place: i for i, place in enumerate(places)}

    def pairs(move, chosen=lambda g, z, s, c: True):
        return [(index[p], index[move(*p)]) for p in places if chosen(*p)]

    def is_home(g, z, s, c):
        return z // 2 == s

    def is_away(g, z, s, c):
        return z // 2 != s

    def jumped(g, z, s, c):
        return (g, z ^ 2, s, c)

    cross_pairs = pairs(lambda g, z, s, c: (g, z, 1 - s, c))
    step_pairs = pairs(lambda g, z, s, c: (g, z ^ 1, s, c))
    core_pairs = pairs(lambda g, z, s, c: (g, z, s, 1 - c))
    home_jump_pairs, away_jump_pairs = pairs(jumped, is_home), pairs(jumped, is_away)

    def cross(a):
        return lax.ppermute(a, AXES, cross_pairs)

    def step(a):
        return lax.ppermute(a, AXES, step_pairs)

    def swap(a):
        return lax.ppermute(a, AXES, core_pairs)

    def home_jump(a):
        return lax.ppermute(a, AXES, home_jump_pairs)

    def away_jump(a):
        return lax.ppermute(a, AXES, away_jump_pairs)

    def shards(expected_cot, value_next, transition, section):
        df = factor_of(section)
        z, s, c = lax.axis_index("markov"), lax.axis_index("storage"), lax.axis_index("sub")
        home = z // 2 == s
        mine = z % 2 == c
        half = expected_cot.shape[1] // 2
        ep, eq = expected_cot[:, :half], expected_cot[:, half:]
        vp, vq = value_next[:, :half], value_next[:, half:]

        x1 = cross(jnp.where(home, vp, ep))
        jq = away_jump(eq)
        t_other = swap(transition)
        v_other = swap(value_next)
        vp2, vq2 = lax.optimization_barrier((vp, vq, x1))[:2]
        x2 = cross(jnp.where(home, vq2, vp2))
        jp = home_jump(x1)
        vq3, jq3 = lax.optimization_barrier((vq, jq, x2))[:2]
        x3 = cross(jnp.where(home, jq3, vq3))
        jq2 = away_jump(x3)
        bp = jnp.where(home, x1, after(jp, x3))
        bp_next = step(bp)
        jap = home_jump(after(ep, jp, x3))
        t_other = after(t_other, x2)
        t_near, t_next = jnp.where(mine, transition, t_other), jnp.where(mine, t_other, transition)

        def adjoint_of(near, far):
            return tdot(t_near, near) + tdot(t_next, far)

        part_p = cross(adjoint_of(bp, bp_next))
        jq2_late, x3_late = lax.optimization_barrier((jq2, x3, bp_next))[:2]
        bq = jnp.where(home, jq2_late, x3_late)
        bq_next = step(bq)
        jaq = home_jump(after(eq, jap, bp_next, jq2))
        ep_late, jap_late = lax.optimization_barrier((ep, jap, bq_next))[:2]
        ap = jnp.where(home, ep_late, jap_late)
        ap_next = step(ap)
        part_q = cross(after(adjoint_of(bq, bq_next), part_p))
        eq_late, jaq_late = lax.optimization_barrier((eq, jaq, ap_next))[:2]
        aq = jnp.where(home, eq_late, jaq_late)
        aq_next = step(aq)

        v_across = jnp.concatenate([jnp.where(home, x2, x1), jnp.where(home, x3, x2)], 1)
        v_across_other = swap(after(v_across, bp_next))

        def own_and_swapped(near, far):
            return jnp.where(mine, near, far), swap(jnp.where(mine, far, near))

        bp_own, bp_swapped = own_and_swapped(bp, bp_next)
        bq_own, bq_swapped = own_and_swapped(bq, bq_next)
        grad = dott(
            jnp.concatenate([bp_own, bq_own, bp_swapped, bq_swapped], 1),
            jnp.concatenate([v_across, v_across_other], 1),
        )
        ap_own, ap_swapped = own_and_swapped(ap, ap_next)
        aq_near, aq_far = lax.optimization_barrier((aq, aq_next, grad))[:2]
        aq_own, aq_swapped = own_and_swapped(aq_near, aq_far)
        grad = grad + dott(
            jnp.concatenate([ap_own, aq_own, ap_swapped, aq_swapped], 1),
            jnp.concatenate([value_next, v_other], 1),
        )
        adjoint = jnp.concatenate([adjoint_of(ap, ap_next) + part_p, adjoint_of(aq, aq_next) + part_q], 1)
        return df * adjoint, df * grad

    return shards


def solution(mesh):
    sizes = tuple(mesh.shape[a] for a in AXES)
    shards = two_side_shards(sizes) if sizes[1:] == (4, 2, 2) else plain_shards
    return jax.shard_map(
        shards,
        mesh=mesh,
        in_specs=(
            P(("groups", "markov"), ("storage", "sub")),
            P(("groups", "markov"), ("storage", "sub")),
            P(("groups", "storage", "sub"), "markov"),
            P("groups"),
        ),
        out_specs=(
            P(("groups", "markov"), ("storage", "sub")),
            P(("groups", "storage", "sub"), "markov"),
        ),
        check_vma=False,
    )
```

```python
import jax
import jax.numpy as jnp
from jax import lax
from jax.sharding import PartitionSpec as P

discount_rate = 0.97
AXES = ("groups", "markov", "storage", "sub")


def factor_of(section):
    return jnp.exp(section[0].astype(jnp.float32) * jnp.log(jnp.float32(discount_rate)))


def plain_shards(expected_cot, value_next, transition, section):
    discount_factor = factor_of(section)
    cotangent_all = lax.all_gather(expected_cot, "markov", axis=0, tiled=True)
    adjoint_sum = lax.dot_general(
        lax.all_gather(transition, ("storage", "sub"), axis=0, tiled=True),
        cotangent_all,
        (((0,), (0,)), ((), ())),
        preferred_element_type=jnp.float32,
    )
    own_states = lax.all_to_all(
        cotangent_all, ("storage", "sub"), split_axis=0, concat_axis=1, tiled=True
    )
    gathered_values = lax.all_gather(value_next, ("storage", "sub"), axis=1, tiled=True)
    gradient_sum = lax.dot_general(
        own_states, gathered_values, (((1,), (1,)), ((), ())), preferred_element_type=jnp.float32
    )
    return (discount_factor * adjoint_sum, discount_factor * gradient_sum)


def tdot(a, b):
    return lax.dot_general(a, b, (((0,), (0,)), ((), ())), preferred_element_type=jnp.float32)


def dott(a, b):
    return lax.dot_general(a, b, (((1,), (1,)), ((), ())), preferred_element_type=jnp.float32)


def after(array, *others):
    return lax.optimization_barrier((array,) + others)[0]


def two_side_shards(sizes):
    groups, layers, sides, cores = sizes
    places = [(g, z, s, c) for g in range(groups) for z in range(layers) for s in range(sides) for c in range(cores)]
    index = {place: i for i, place in enumerate(places)}

    def pairs(move, chosen=lambda g, z, s, c: True):
        return [(index[p], index[move(*p)]) for p in places if chosen(*p)]

    def is_home(g, z, s, c):
        return z // 2 == s

    def is_away(g, z, s, c):
        return z // 2 != s

    def jumped(g, z, s, c):
        return (g, z ^ 2, s, c)

    cross_pairs = pairs(lambda g, z, s, c: (g, z, 1 - s, c))
    step_pairs = pairs(lambda g, z, s, c: (g, z ^ 1, s, c))
    core_pairs = pairs(lambda g, z, s, c: (g, z, s, 1 - c))
    home_jump_pairs, away_jump_pairs = pairs(jumped, is_home), pairs(jumped, is_away)

    def cross(a):
        return lax.ppermute(a, AXES, cross_pairs)

    def step(a):
        return lax.ppermute(a, AXES, step_pairs)

    def swap(a):
        return lax.ppermute(a, AXES, core_pairs)

    def home_jump(a):
        return lax.ppermute(a, AXES, home_jump_pairs)

    def away_jump(a):
        return lax.ppermute(a, AXES, away_jump_pairs)

    def shards(expected_cot, value_next, transition, section):
        df = factor_of(section)
        z, s, c = lax.axis_index("markov"), lax.axis_index("storage"), lax.axis_index("sub")
        home = z // 2 == s
        mine = z % 2 == c
        half = expected_cot.shape[1] // 2
        quarter = half // 2

        def columns(array, start, stop):
            return array[:, start * quarter : stop * quarter]

        def together(arrays, *gates):
            return lax.optimization_barrier(tuple(arrays) + gates)[: len(arrays)]

        e_1, e_q = columns(expected_cot, 0, 1), columns(expected_cot, 2, 4)
        first, e_1, e_q = together((jnp.where(home, columns(value_next, 0, 1), e_1), e_1, e_q))
        c1 = cross(first)
        ja1 = home_jump(e_1)
        jq = away_jump(e_q)
        v, e = together((columns(value_next, 1, 2), columns(expected_cot, 1, 2)), c1)
        c2 = cross(jnp.where(home, v, e))
        jp1 = home_jump(after(c1, ja1))
        t_other = swap(after(transition, c1))
        jq_late, vp = together((jq, columns(value_next, 0, 2)), c2)
        c3 = cross(jnp.where(home, jq_late, vp))
        x, j = together((c1, jp1), c2)
        b1 = jnp.where(home, x, j)
        b1_next = step(b1)
        jp2 = home_jump(after(c2, jp1))
        jq2 = away_jump(c3)
        t, t_o = together((transition, t_other), b1_next)
        t_near, t_next = jnp.where(mine, t, t_o), jnp.where(mine, t_o, t)

        def adjoint_of(near, far):
            return tdot(t_near, near) + tdot(t_next, far)

        part1 = cross(after(adjoint_of(b1, b1_next), c3))
        c4 = cross(after(columns(value_next, 2, 4), c3))
        x, j = together((c2, jp2), b1_next)
        b2 = jnp.where(home, x, j)
        b2_next = step(b2)
        ja2 = home_jump(after(columns(expected_cot, 1, 4), jp2, b1_next))
        e, j = together((columns(expected_cot, 0, 1), ja1), b2_next)
        a1 = jnp.where(home, e, j)
        a1_next = step(a1)
        part2 = cross(after(adjoint_of(b2, b2_next), part1, c4))
        j, x = together((jq2, c3), a1_next, part1)
        bq = jnp.where(home, j, x)
        bq_next = step(bq)
        v_other = swap(after(value_next, b2_next))
        sum3 = adjoint_of(bq, bq_next)
        part3 = cross(after(columns(sum3, 0, 1), part2))
        part4 = cross(after(columns(sum3, 1, 2), part3))
        e, j = together((columns(expected_cot, 1, 4), ja2), bq_next, part2, sum3)
        a2 = jnp.where(home, e, j)
        a2_next = step(a2)

        def own_and_swapped(near, far):
            return jnp.where(mine, near, far), swap(jnp.where(mine, far, near))

        v_across = jnp.concatenate([jnp.where(home, c3, jnp.concatenate([c1, c2], 1)), c4], 1)
        v_across_other = swap(after(v_across, b2_next))
        bp_own, bp_swapped = own_and_swapped(
            jnp.concatenate([b1, b2], 1), jnp.concatenate([b1_next, b2_next], 1)
        )
        bq_own, bq_swapped = own_and_swapped(bq, bq_next)
        grad = dott(
            jnp.concatenate([bp_own, bq_own, bp_swapped, bq_swapped], 1),
            jnp.concatenate([v_across, v_across_other], 1),
        )
        a1_own, a1_swapped = own_and_swapped(a1, a1_next)
        a2_near, a2_far = together((a2, a2_next), grad, part3)
        a2_own, a2_swapped = own_and_swapped(a2_near, a2_far)
        grad = df * (grad + dott(
            jnp.concatenate([a1_own, a2_own, a1_swapped, a2_swapped], 1),
            jnp.concatenate([value_next, v_other], 1),
        ))
        own = adjoint_of(jnp.concatenate([a1, a2], 1), jnp.concatenate([a1_next, a2_next], 1))
        own, part4, grad = together((own, part4, grad))
        adjoint = df * (own + jnp.concatenate([part1, part2, part3, part4], 1))
        return adjoint, grad

    return shards


def solution(mesh):
    sizes = tuple(mesh.shape[a] for a in AXES)
    shards = two_side_shards(sizes) if sizes[1:] == (4, 2, 2) else plain_shards
    return jax.shard_map(
        shards,
        mesh=mesh,
        in_specs=(
            P(("groups", "markov"), ("storage", "sub")),
            P(("groups", "markov"), ("storage", "sub")),
            P(("groups", "storage", "sub"), "markov"),
            P("groups"),
        ),
        out_specs=(
            P(("groups", "markov"), ("storage", "sub")),
            P(("groups", "storage", "sub"), "markov"),
        ),
        check_vma=False,
    )
```

```python
import jax
import jax.numpy as jnp
from jax import lax
from jax.sharding import PartitionSpec as P

discount_rate = 0.97
AXES = ("groups", "markov", "storage", "sub")


def factor_of(section):
    return jnp.exp(section[0].astype(jnp.float32) * jnp.log(jnp.float32(discount_rate)))


def plain_shards(expected_cot, value_next, transition, section):
    discount_factor = factor_of(section)
    cotangent_all = lax.all_gather(expected_cot, "markov", axis=0, tiled=True)
    adjoint_sum = lax.dot_general(
        lax.all_gather(transition, ("storage", "sub"), axis=0, tiled=True),
        cotangent_all,
        (((0,), (0,)), ((), ())),
        preferred_element_type=jnp.float32,
    )
    own_states = lax.all_to_all(
        cotangent_all, ("storage", "sub"), split_axis=0, concat_axis=1, tiled=True
    )
    gathered_values = lax.all_gather(value_next, ("storage", "sub"), axis=1, tiled=True)
    gradient_sum = lax.dot_general(
        own_states, gathered_values, (((1,), (1,)), ((), ())), preferred_element_type=jnp.float32
    )
    return (discount_factor * adjoint_sum, discount_factor * gradient_sum)


def tdot(a, b):
    return lax.dot_general(a, b, (((0,), (0,)), ((), ())), preferred_element_type=jnp.float32)


def dott(a, b):
    return lax.dot_general(a, b, (((1,), (1,)), ((), ())), preferred_element_type=jnp.float32)


def after(array, *others):
    return lax.optimization_barrier((array,) + others)[0]


def two_side_shards(sizes):
    groups, layers, sides, cores = sizes
    places = [(g, z, s, c) for g in range(groups) for z in range(layers) for s in range(sides) for c in range(cores)]
    index = {place: i for i, place in enumerate(places)}

    def pairs(move, chosen=lambda g, z, s, c: True):
        return [(index[p], index[move(*p)]) for p in places if chosen(*p)]

    def is_home(g, z, s, c):
        return z // 2 == s

    def jumped(g, z, s, c):
        return (g, z ^ 2, s, c)

    cross_pairs = pairs(lambda g, z, s, c: (g, z, 1 - s, c))
    step_pairs = pairs(lambda g, z, s, c: (g, z ^ 1, s, c))
    core_pairs = pairs(lambda g, z, s, c: (g, z, s, 1 - c))
    jump_pairs, home_jump_pairs = pairs(jumped), pairs(jumped, is_home)

    def cross(a):
        return lax.ppermute(a, AXES, cross_pairs)

    def step(a):
        return lax.ppermute(a, AXES, step_pairs)

    def swap(a):
        return lax.ppermute(a, AXES, core_pairs)

    def home_jump(a):
        return lax.ppermute(a, AXES, home_jump_pairs)

    def jump(a):
        return lax.ppermute(a, AXES, jump_pairs)

    def shards(expected_cot, value_next, transition, section):
        df = factor_of(section)
        z, s, c = lax.axis_index("markov"), lax.axis_index("storage"), lax.axis_index("sub")
        home = z // 2 == s
        mine = z % 2 == c
        half = expected_cot.shape[1] // 2
        quarter = half // 2

        def columns(array, start, stop):
            return array[:, start * quarter : stop * quarter]

        def together(arrays, *gates):
            return lax.optimization_barrier(tuple(arrays) + gates)[: len(arrays)]

        e = [columns(expected_cot, i, i + 1) for i in range(4)]
        v = [columns(value_next, i, i + 1) for i in range(4)]
        first_cross, first_jump, e3 = together(
            (jnp.where(home, v[0], e[0]), jnp.where(home, e[0], e[2]), e[3])
        )
        x1 = cross(first_cross)
        j1 = jump(first_jump)
        v1, e1 = together((v[1], e[1]), x1, j1)
        x2 = cross(jnp.where(home, v1, e1))
        near, far = together((x1, e3), j1)
        j2 = jump(jnp.where(home, near, far))
        t_other = swap(after(transition, j1))
        near, far = together((j1, v[0]), x2)
        x3 = cross(jnp.where(home, near, far))
        t, t_o = together((transition, t_other), x2)
        t_near, t_next = jnp.where(mine, t, t_o), jnp.where(mine, t_o, t)

        def adjoint_of(near, far):
            return tdot(t_near, near) + tdot(t_next, far)

        near, far = together((x2, x3), j2)
        j3 = jump(jnp.where(home, near, far))
        near, far = together((j2, v[1]), x3)
        x4 = cross(jnp.where(home, near, far))
        near, far = together((x1, j2), x3, t_near)
        b0 = jnp.where(home, near, far)
        b0_next = step(b0)
        x5 = cross(after(columns(value_next, 2, 4), x4, b0_next))
        near, far = together((e[1], x4), j3, b0_next)
        j4 = jump(jnp.where(home, near, far))
        sum0 = adjoint_of(b0, b0_next)
        part0 = cross(after(sum0, x4))
        near, far = together((x2, j3), sum0, x4)
        b1 = jnp.where(home, near, far)
        b1_next = step(b1)
        part1 = cross(after(adjoint_of(b1, b1_next), x5, part0))
        near, far = together((j3, x3), b1_next)
        b2 = jnp.where(home, near, far)
        b2_next = step(b2)
        part2 = cross(after(adjoint_of(b2, b2_next), part1))
        near, far = together((j4, x4), b2_next, part0, x5)
        b3 = jnp.where(home, near, far)
        b3_next = step(b3)
        part3 = cross(after(adjoint_of(b3, b3_next), part2))
        j5 = home_jump(after(columns(expected_cot, 2, 4), j4))
        v_other = swap(after(value_next, b1_next))
        near, far = together((columns(expected_cot, 0, 2), jnp.concatenate([j1, j4], 1)), b3_next, part1)
        a01 = jnp.where(home, near, far)
        a01_next = step(a01)

        def own_and_swapped(near, far):
            return jnp.where(mine, near, far), swap(jnp.where(mine, far, near))

        v_across = jnp.concatenate(
            [jnp.where(home, jnp.concatenate([x3, x4], 1), jnp.concatenate([x1, x2], 1)), x5], 1
        )
        v_across_other = swap(after(v_across, b1_next))
        b_own, b_swapped = own_and_swapped(
            jnp.concatenate([b0, b1, b2, b3], 1),
            jnp.concatenate([b0_next, b1_next, b2_next, b3_next], 1),
        )
        grad = dott(
            jnp.concatenate([b_own, b_swapped], 1), jnp.concatenate([v_across, v_across_other], 1)
        )
        a01_own, a01_swapped = own_and_swapped(a01, a01_next)
        near, far = together((columns(expected_cot, 2, 4), j5), a01_next, part2)
        a23 = jnp.where(home, near, far)
        a23_next = step(a23)
        near, far = together((a23, a23_next), grad)
        a23_own, a23_swapped = own_and_swapped(near, far)
        grad = df * (grad + dott(
            jnp.concatenate([a01_own, a23_own, a01_swapped, a23_swapped], 1),
            jnp.concatenate([value_next, v_other], 1),
        ))
        own = adjoint_of(jnp.concatenate([a01, a23], 1), jnp.concatenate([a01_next, a23_next], 1))
        own, part3, grad = together((own, part3, grad))
        adjoint = df * (own + jnp.concatenate([part0, part1, part2, part3], 1))
        return adjoint, grad

    return shards


def solution(mesh):
    sizes = tuple(mesh.shape[a] for a in AXES)
    shards = two_side_shards(sizes) if sizes[1:] == (4, 2, 2) else plain_shards
    return jax.shard_map(
        shards,
        mesh=mesh,
        in_specs=(
            P(("groups", "markov"), ("storage", "sub")),
            P(("groups", "markov"), ("storage", "sub")),
            P(("groups", "storage", "sub"), "markov"),
            P("groups"),
        ),
        out_specs=(
            P(("groups", "markov"), ("storage", "sub")),
            P(("groups", "storage", "sub"), "markov"),
        ),
        check_vma=False,
    )
```

```python
import jax
import jax.numpy as jnp
from jax import lax
from jax.sharding import PartitionSpec as P

discount_rate = 0.97
AXES = ("groups", "markov", "storage", "sub")


def factor_of(section):
    return jnp.exp(section[0].astype(jnp.float32) * jnp.log(jnp.float32(discount_rate)))


def plain_shards(expected_cot, value_next, transition, section):
    discount_factor = factor_of(section)
    cotangent_all = lax.all_gather(expected_cot, "markov", axis=0, tiled=True)
    adjoint_sum = lax.dot_general(
        lax.all_gather(transition, ("storage", "sub"), axis=0, tiled=True),
        cotangent_all,
        (((0,), (0,)), ((), ())),
        preferred_element_type=jnp.float32,
    )
    own_states = lax.all_to_all(
        cotangent_all, ("storage", "sub"), split_axis=0, concat_axis=1, tiled=True
    )
    gathered_values = lax.all_gather(value_next, ("storage", "sub"), axis=1, tiled=True)
    gradient_sum = lax.dot_general(
        own_states, gathered_values, (((1,), (1,)), ((), ())), preferred_element_type=jnp.float32
    )
    return (discount_factor * adjoint_sum, discount_factor * gradient_sum)


def tdot(a, b):
    return lax.dot_general(a, b, (((0,), (0,)), ((), ())), preferred_element_type=jnp.float32)


def dott(a, b):
    return lax.dot_general(a, b, (((1,), (1,)), ((), ())), preferred_element_type=jnp.float32)


def after(array, *others):
    return lax.optimization_barrier((array,) + others)[0]


def two_side_shards(sizes):
    groups, layers, sides, cores = sizes
    places = [(g, z, s, c) for g in range(groups) for z in range(layers) for s in range(sides) for c in range(cores)]
    index = {place: i for i, place in enumerate(places)}

    def pairs(move, chosen=lambda g, z, s, c: True):
        return [(index[p], index[move(*p)]) for p in places if chosen(*p)]

    def is_home(g, z, s, c):
        return z // 2 == s

    def jumped(g, z, s, c):
        return (g, z ^ 2, s, c)

    cross_pairs = pairs(lambda g, z, s, c: (g, z, 1 - s, c))
    step_pairs = pairs(lambda g, z, s, c: (g, z ^ 1, s, c))
    core_pairs = pairs(lambda g, z, s, c: (g, z, s, 1 - c))
    jump_pairs, home_jump_pairs = pairs(jumped), pairs(jumped, is_home)

    def cross(a):
        return lax.ppermute(a, AXES, cross_pairs)

    def step(a):
        return lax.ppermute(a, AXES, step_pairs)

    def swap(a):
        return lax.ppermute(a, AXES, core_pairs)

    def home_jump(a):
        return lax.ppermute(a, AXES, home_jump_pairs)

    def jump(a):
        return lax.ppermute(a, AXES, jump_pairs)

    def shards(expected_cot, value_next, transition, section):
        df = factor_of(section)
        z, s, c = lax.axis_index("markov"), lax.axis_index("storage"), lax.axis_index("sub")
        home = z // 2 == s
        mine = z % 2 == c
        half = expected_cot.shape[1] // 2
        quarter = half // 2

        def columns(array, start, stop):
            return array[:, start * quarter : stop * quarter]

        def together(arrays, *gates):
            return lax.optimization_barrier(tuple(arrays) + gates)[: len(arrays)]

        e = [columns(expected_cot, i, i + 1) for i in range(4)]
        v = [columns(value_next, i, i + 1) for i in range(4)]
        first_cross, first_jump, e3 = together(
            (jnp.concatenate([jnp.where(home, v[0], e[0]), v[2]], 1), jnp.where(home, e[0], e[2]), e[3])
        )
        x1 = cross(first_cross)
        x1, v_across2 = columns(x1, 0, 1), columns(x1, 1, 2)
        j1 = jump(first_jump)
        v1, e1 = together((v[1], e[1]), x1, j1)
        x2 = cross(jnp.where(home, v1, e1))
        near, far = together((x1, e3), j1)
        j2 = jump(jnp.where(home, near, far))
        t_other = swap(transition)
        near, far = together((j1, v[0]), x2)
        x3 = cross(jnp.where(home, near, far))
        t, t_o = together((transition, t_other), x3)
        t_near, t_next = jnp.where(mine, t, t_o), jnp.where(mine, t_o, t)

        def adjoint_of(near, far):
            return tdot(t_near, near) + tdot(t_next, far)

        near, far = together((x2, x3), j2)
        j3 = jump(jnp.where(home, near, far))
        near, far = together((j2, v[1]), x3)
        x4 = cross(jnp.concatenate([jnp.where(home, near, far), v[3]], 1))
        x4, v_across3 = columns(x4, 0, 1), columns(x4, 1, 2)
        near, far = together((x1, j2), x3, t_near)
        b0 = jnp.where(home, near, far)
        b0_next = step(b0)
        near, far = together((e[1], x4), j3, b0_next)
        j4 = jump(jnp.where(home, near, far))
        sum0 = adjoint_of(b0, b0_next)
        part0 = cross(after(sum0, x4))
        near, far = together((x2, j3), sum0, x4)
        b1 = jnp.where(home, near, far)
        b1_next = step(b1)
        part1 = cross(after(adjoint_of(b1, b1_next), part0))
        near, far = together((j3, x3), b1_next)
        b2 = jnp.where(home, near, far)
        b2_next = step(b2)
        part2 = cross(after(adjoint_of(b2, b2_next), part1))
        near, far = together((j4, x4), b2_next, part0)
        b3 = jnp.where(home, near, far)
        b3_next = step(b3)
        part3 = cross(after(adjoint_of(b3, b3_next), part2))
        j5 = home_jump(after(columns(expected_cot, 2, 4), j4))
        v_other = swap(after(value_next, b1_next))
        near, far = together((columns(expected_cot, 0, 2), jnp.concatenate([j1, j4], 1)), b3_next, part1)
        a01 = jnp.where(home, near, far)
        a01_next = step(a01)

        def own_and_swapped(near, far):
            return jnp.where(mine, near, far), swap(jnp.where(mine, far, near))

        v_across = jnp.concatenate(
            [jnp.where(home, jnp.concatenate([x3, x4], 1), jnp.concatenate([x1, x2], 1)), v_across2, v_across3],
            1,
        )
        v_across_other = swap(after(v_across, b1_next))
        b_own, b_swapped = own_and_swapped(
            jnp.concatenate([b0, b1, b2, b3], 1),
            jnp.concatenate([b0_next, b1_next, b2_next, b3_next], 1),
        )
        grad = dott(
            jnp.concatenate([b_own, b_swapped], 1), jnp.concatenate([v_across, v_across_other], 1)
        )
        a01_own, a01_swapped = own_and_swapped(a01, a01_next)
        near, far = together((columns(expected_cot, 2, 4), j5), a01_next, part2)
        a23 = jnp.where(home, near, far)
        a23_next = step(a23)
        near, far = together((a23, a23_next), grad)
        a23_own, a23_swapped = own_and_swapped(near, far)
        grad = df * (grad + dott(
            jnp.concatenate([a01_own, a23_own, a01_swapped, a23_swapped], 1),
            jnp.concatenate([value_next, v_other], 1),
        ))
        own = adjoint_of(jnp.concatenate([a01, a23], 1), jnp.concatenate([a01_next, a23_next], 1))
        own, part3, grad = together((own, part3, grad))
        adjoint = df * (own + jnp.concatenate([part0, part1, part2, part3], 1))
        return adjoint, grad

    return shards


def solution(mesh):
    sizes = tuple(mesh.shape[a] for a in AXES)
    shards = two_side_shards(sizes) if sizes[1:] == (4, 2, 2) else plain_shards
    return jax.shard_map(
        shards,
        mesh=mesh,
        in_specs=(
            P(("groups", "markov"), ("storage", "sub")),
            P(("groups", "markov"), ("storage", "sub")),
            P(("groups", "storage", "sub"), "markov"),
            P("groups"),
        ),
        out_specs=(
            P(("groups", "markov"), ("storage", "sub")),
            P(("groups", "storage", "sub"), "markov"),
        ),
        check_vma=False,
    )
```

```python
import jax
import jax.numpy as jnp
from jax import lax
from jax.sharding import PartitionSpec as P

discount_rate = 0.97
AXES = ("groups", "markov", "storage", "sub")


def factor_of(section):
    return jnp.exp(section[0].astype(jnp.float32) * jnp.log(jnp.float32(discount_rate)))


def plain_shards(expected_cot, value_next, transition, section):
    discount_factor = factor_of(section)
    cotangent_all = lax.all_gather(expected_cot, "markov", axis=0, tiled=True)
    adjoint_sum = lax.dot_general(
        lax.all_gather(transition, ("storage", "sub"), axis=0, tiled=True),
        cotangent_all,
        (((0,), (0,)), ((), ())),
        preferred_element_type=jnp.float32,
    )
    own_states = lax.all_to_all(
        cotangent_all, ("storage", "sub"), split_axis=0, concat_axis=1, tiled=True
    )
    gathered_values = lax.all_gather(value_next, ("storage", "sub"), axis=1, tiled=True)
    gradient_sum = lax.dot_general(
        own_states, gathered_values, (((1,), (1,)), ((), ())), preferred_element_type=jnp.float32
    )
    return (discount_factor * adjoint_sum, discount_factor * gradient_sum)


def tdot(a, b):
    return lax.dot_general(a, b, (((0,), (0,)), ((), ())), preferred_element_type=jnp.float32)


def dott(a, b):
    return lax.dot_general(a, b, (((1,), (1,)), ((), ())), preferred_element_type=jnp.float32)


def after(array, *others):
    return lax.optimization_barrier((array,) + others)[0]


def two_side_shards(sizes):
    groups, layers, sides, cores = sizes
    places = [(g, z, s, c) for g in range(groups) for z in range(layers) for s in range(sides) for c in range(cores)]
    index = {place: i for i, place in enumerate(places)}

    def pairs(move, chosen=lambda g, z, s, c: True):
        return [(index[p], index[move(*p)]) for p in places if chosen(*p)]

    def is_home(g, z, s, c):
        return z // 2 == s

    def jumped(g, z, s, c):
        return (g, z ^ 2, s, c)

    cross_pairs = pairs(lambda g, z, s, c: (g, z, 1 - s, c))
    step_pairs = pairs(lambda g, z, s, c: (g, z ^ 1, s, c))
    core_pairs = pairs(lambda g, z, s, c: (g, z, s, 1 - c))
    jump_pairs, home_jump_pairs = pairs(jumped), pairs(jumped, is_home)

    def cross(a):
        return lax.ppermute(a, AXES, cross_pairs)

    def step(a):
        return lax.ppermute(a, AXES, step_pairs)

    def swap(a):
        return lax.ppermute(a, AXES, core_pairs)

    def home_jump(a):
        return lax.ppermute(a, AXES, home_jump_pairs)

    def jump(a):
        return lax.ppermute(a, AXES, jump_pairs)

    def shards(expected_cot, value_next, transition, section):
        df = factor_of(section)
        z, s, c = lax.axis_index("markov"), lax.axis_index("storage"), lax.axis_index("sub")
        home = z // 2 == s
        mine = z % 2 == c
        half = expected_cot.shape[1] // 2
        quarter = half // 2

        def columns(array, start, stop):
            return array[:, start * quarter : stop * quarter]

        def together(arrays, *gates):
            return lax.optimization_barrier(tuple(arrays) + gates)[: len(arrays)]

        e = [columns(expected_cot, i, i + 1) for i in range(4)]
        v = [columns(value_next, i, i + 1) for i in range(4)]
        first_cross, first_jump, e3 = together(
            (jnp.concatenate([jnp.where(home, v[0], e[0]), v[2]], 1), jnp.where(home, e[0], e[2]), e[3])
        )
        x1 = cross(first_cross)
        x1, v_across2 = columns(x1, 0, 1), columns(x1, 1, 2)
        j1 = jump(first_jump)
        v1, e1 = together((v[1], e[1]), x1, j1)
        x2 = cross(jnp.where(home, v1, e1))
        near, far = together((x1, e3), j1)
        j2 = jump(jnp.where(home, near, far))
        a0 = jnp.where(home, e[0], j1)
        a0_next = step(a0)
        t_other = swap(transition)
        near, far = together((j1, v[0]), x2)
        x3 = cross(jnp.where(home, near, far))
        t, t_o = together((transition, t_other), x2)
        t_near, t_next = jnp.where(mine, t, t_o), jnp.where(mine, t_o, t)

        def adjoint_of(near, far):
            return tdot(t_near, near) + tdot(t_next, far)

        near, far = together((x2, x3), j2)
        j3 = jump(jnp.where(home, near, far))
        near, far = together((x1, j2), t_near, a0_next)
        b0 = jnp.where(home, near, far)
        b0_next = step(b0)
        near, far = together((j2, v[1]), x3, b0)
        x4 = cross(jnp.concatenate([jnp.where(home, near, far), v[3]], 1))
        x4, v_across3 = columns(x4, 0, 1), columns(x4, 1, 2)
        near, far = together((e[1], x4), j3)
        j4 = jump(jnp.where(home, near, far))
        sum0 = adjoint_of(b0, b0_next)
        part0 = cross(after(sum0, x4))
        near, both, far = together((x2, j3, x3), sum0)
        b12 = jnp.where(home, jnp.concatenate([near, both], 1), jnp.concatenate([both, far], 1))
        b12_next = step(b12)
        sum12 = adjoint_of(b12, b12_next)
        sum1, sum2 = columns(sum12, 0, 1), columns(sum12, 1, 2)
        part1 = cross(after(sum1, part0))
        part2 = cross(after(sum2, part1))
        j5 = home_jump(after(e[2], j4))
        near, both, far = together((e[1], j4, x4), sum12, part0)
        a1b3 = jnp.where(home, jnp.concatenate([near, both], 1), jnp.concatenate([both, far], 1))
        a1b3_next = step(a1b3)
        j6 = home_jump(after(e[3], j5, part1))
        v_other = swap(after(value_next, sum12))
        sum3 = adjoint_of(columns(a1b3, 1, 2), columns(a1b3_next, 1, 2))
        part3 = cross(after(sum3, part2))

        def own_and_swapped(near, far):
            return jnp.where(mine, near, far), swap(jnp.where(mine, far, near))

        parts = together((x1, x2, x3, x4, v_across2, v_across3), sum12)
        v_across = jnp.concatenate(
            [jnp.where(home, parts[2], parts[0]), jnp.where(home, parts[3], parts[1]), parts[4], parts[5]], 1
        )
        v_across_other = swap(v_across)
        a0, a0_next, b0, b0_next, b12, b12_next = together((a0, a0_next, b0, b0_next, b12, b12_next), a1b3_next, sum3, part2)
        a1, a1_next = columns(a1b3, 0, 1), columns(a1b3_next, 0, 1)
        b_own, b_swapped = own_and_swapped(
            jnp.concatenate([b0, b12, columns(a1b3, 1, 2)], 1),
            jnp.concatenate([b0_next, b12_next, columns(a1b3_next, 1, 2)], 1),
        )
        a01_own, a01_swapped = own_and_swapped(
            jnp.concatenate([a0, a1], 1), jnp.concatenate([a0_next, a1_next], 1)
        )
        grad = dott(
            jnp.concatenate([b_own, b_swapped], 1), jnp.concatenate([v_across, v_across_other], 1)
        ) + dott(
            jnp.concatenate([a01_own, a01_swapped], 1),
            jnp.concatenate([columns(value_next, 0, 2), columns(v_other, 0, 2)], 1),
        )
        near, far = together((e[2], j5), a1b3_next, sum3, part1)
        a2 = jnp.where(home, near, far)
        a2_next = step(a2)
        own01 = adjoint_of(jnp.concatenate([a0, a1], 1), jnp.concatenate([a0_next, a1_next], 1))
        near, far = together((e[3], j6), grad, own01, a2_next, part2)
        a3 = jnp.where(home, near, far)
        a3_next = step(a3)
        a2_own, a2_swapped = own_and_swapped(a2, a2_next)
        a3_own, a3_swapped = own_and_swapped(a3, a3_next)
        grad = df * (grad + dott(
            jnp.concatenate([a2_own, a3_own, a2_swapped, a3_swapped], 1),
            jnp.concatenate([columns(value_next, 2, 4), columns(v_other, 2, 4)], 1),
        ))
        own23 = adjoint_of(jnp.concatenate([a2, a3], 1), jnp.concatenate([a2_next, a3_next], 1))
        own23, part3, grad = together((own23, part3, grad))
        adjoint = df * (
            jnp.concatenate([own01, own23], 1) + jnp.concatenate([part0, part1, part2, part3], 1)
        )
        return adjoint, grad

    return shards


def solution(mesh):
    sizes = tuple(mesh.shape[a] for a in AXES)
    shards = two_side_shards(sizes) if sizes[1:] == (4, 2, 2) else plain_shards
    return jax.shard_map(
        shards,
        mesh=mesh,
        in_specs=(
            P(("groups", "markov"), ("storage", "sub")),
            P(("groups", "markov"), ("storage", "sub")),
            P(("groups", "storage", "sub"), "markov"),
            P("groups"),
        ),
        out_specs=(
            P(("groups", "markov"), ("storage", "sub")),
            P(("groups", "storage", "sub"), "markov"),
        ),
        check_vma=False,
    )
```

```python
import jax
import jax.numpy as jnp
from jax import lax
from jax.sharding import PartitionSpec as P

discount_rate = 0.97
AXES = ("groups", "markov", "storage", "sub")


def factor_of(section):
    return jnp.exp(section[0].astype(jnp.float32) * jnp.log(jnp.float32(discount_rate)))


def plain_shards(expected_cot, value_next, transition, section):
    discount_factor = factor_of(section)
    cotangent_all = lax.all_gather(expected_cot, "markov", axis=0, tiled=True)
    adjoint_sum = lax.dot_general(
        lax.all_gather(transition, ("storage", "sub"), axis=0, tiled=True),
        cotangent_all,
        (((0,), (0,)), ((), ())),
        preferred_element_type=jnp.float32,
    )
    own_states = lax.all_to_all(
        cotangent_all, ("storage", "sub"), split_axis=0, concat_axis=1, tiled=True
    )
    gathered_values = lax.all_gather(value_next, ("storage", "sub"), axis=1, tiled=True)
    gradient_sum = lax.dot_general(
        own_states, gathered_values, (((1,), (1,)), ((), ())), preferred_element_type=jnp.float32
    )
    return (discount_factor * adjoint_sum, discount_factor * gradient_sum)


def tdot(a, b):
    return lax.dot_general(a, b, (((0,), (0,)), ((), ())), preferred_element_type=jnp.float32)


def dott(a, b):
    return lax.dot_general(a, b, (((1,), (1,)), ((), ())), preferred_element_type=jnp.float32)


def after(array, *others):
    return lax.optimization_barrier((array,) + others)[0]


def two_side_shards(sizes):
    groups, layers, sides, cores = sizes
    places = [(g, z, s, c) for g in range(groups) for z in range(layers) for s in range(sides) for c in range(cores)]
    index = {place: i for i, place in enumerate(places)}

    def pairs(move, chosen=lambda g, z, s, c: True):
        return [(index[p], index[move(*p)]) for p in places if chosen(*p)]

    def is_home(g, z, s, c):
        return z // 2 == s

    def jumped(g, z, s, c):
        return (g, z ^ 2, s, c)

    cross_pairs = pairs(lambda g, z, s, c: (g, z, 1 - s, c))
    step_pairs = pairs(lambda g, z, s, c: (g, z ^ 1, s, c))
    core_pairs = pairs(lambda g, z, s, c: (g, z, s, 1 - c))
    jump_pairs, home_jump_pairs = pairs(jumped), pairs(jumped, is_home)

    def cross(a):
        return lax.ppermute(a, AXES, cross_pairs)

    def step(a):
        return lax.ppermute(a, AXES, step_pairs)

    def swap(a):
        return lax.ppermute(a, AXES, core_pairs)

    def home_jump(a):
        return lax.ppermute(a, AXES, home_jump_pairs)

    def jump(a):
        return lax.ppermute(a, AXES, jump_pairs)

    def shards(expected_cot, value_next, transition, section):
        df = factor_of(section)
        z, s, c = lax.axis_index("markov"), lax.axis_index("storage"), lax.axis_index("sub")
        home = z // 2 == s
        mine = z % 2 == c
        half = expected_cot.shape[1] // 2
        quarter = half // 2

        def columns(array, start, stop):
            return array[:, start * quarter : stop * quarter]

        def together(arrays, *gates):
            return lax.optimization_barrier(tuple(arrays) + gates)[: len(arrays)]

        e = [columns(expected_cot, i, i + 1) for i in range(4)]
        v = [columns(value_next, i, i + 1) for i in range(4)]
        x1 = cross(jnp.where(home, v[0], e[0]))
        t_other = swap(transition)
        e2 = after(e[2], x1)
        j1 = jump(jnp.where(home, x1, e2))
        v1, e1 = together((v[1], e[1]), x1)
        x2 = cross(jnp.concatenate([jnp.where(home, v1, e1), v[2]], 1))
        x2, v_across2 = columns(x2, 0, 1), columns(x2, 1, 2)
        t, t_o = together((transition, t_other), x2)
        t_near, t_next = jnp.where(mine, t, t_o), jnp.where(mine, t_o, t)

        def adjoint_of(near, far):
            return tdot(t_near, near) + tdot(t_next, far)

        near, far = together((x1, j1), x2)
        b0 = jnp.where(home, near, far)
        b0_next = step(b0)
        near, far = together((x2, e[3]), j1, b0)
        j2 = jump(jnp.where(home, near, far))
        near, far = together((j1, v[0]), x2)
        x3 = cross(jnp.concatenate([jnp.where(home, near, far), v[3]], 1))
        x3, v_across3 = columns(x3, 0, 1), columns(x3, 1, 2)
        sum0 = adjoint_of(b0, b0_next)
        part0 = cross(after(sum0, x3))
        near, far = together((e[0], x3), j2, b0_next)
        j3 = jump(jnp.where(home, near, far))
        near, far = together((x2, j2), sum0)
        b1 = jnp.where(home, near, far)
        b1_next = step(b1)
        near, far = together((j2, v[1]), x3, sum0)
        x4 = cross(jnp.where(home, near, far))
        near, far = together((e[1], x4), j3, part0)
        j4 = jump(jnp.where(home, near, far))
        sum1 = adjoint_of(b1, b1_next)
        part1 = cross(after(sum1, part0, x4))
        near, both, far = together((e[0], j3, x3), sum1)
        a0b2 = jnp.where(home, jnp.concatenate([near, both], 1), jnp.concatenate([both, far], 1))
        a0b2_next = step(a0b2)
        sum2 = adjoint_of(columns(a0b2, 1, 2), columns(a0b2_next, 1, 2))
        part2 = cross(after(sum2, part1))
        j5 = home_jump(after(columns(expected_cot, 2, 4), j4))
        near, both, far = together((e[1], j4, x4), sum2, part0)
        a1b3 = jnp.where(home, jnp.concatenate([near, both], 1), jnp.concatenate([both, far], 1))
        a1b3_next = step(a1b3)
        v_other = swap(after(value_next, sum1))
        sum3 = adjoint_of(columns(a1b3, 1, 2), columns(a1b3_next, 1, 2))
        part3 = cross(after(sum3, part2))

        def own_and_swapped(near, far):
            return jnp.where(mine, near, far), swap(jnp.where(mine, far, near))

        parts = together((x1, x2, x3, x4, v_across2, v_across3), sum1)
        v_across = jnp.concatenate(
            [jnp.where(home, parts[2], parts[0]), jnp.where(home, parts[3], parts[1]), parts[4], parts[5]], 1
        )
        v_across_other = swap(v_across)
        near, far = together((columns(expected_cot, 2, 4), j5), a1b3_next, part2)
        a23 = jnp.where(home, near, far)
        a23_next = step(a23)
        b0, b0_next, b1, b1_next, a0b2, a0b2_next = together(
            (b0, b0_next, b1, b1_next, a0b2, a0b2_next), a1b3_next, sum3, part2
        )
        a0, a0_next = columns(a0b2, 0, 1), columns(a0b2_next, 0, 1)
        a1, a1_next = columns(a1b3, 0, 1), columns(a1b3_next, 0, 1)
        b_own, b_swapped = own_and_swapped(
            jnp.concatenate([b0, b1, columns(a0b2, 1, 2), columns(a1b3, 1, 2)], 1),
            jnp.concatenate([b0_next, b1_next, columns(a0b2_next, 1, 2), columns(a1b3_next, 1, 2)], 1),
        )
        a01_own, a01_swapped = own_and_swapped(
            jnp.concatenate([a0, a1], 1), jnp.concatenate([a0_next, a1_next], 1)
        )
        grad = dott(
            jnp.concatenate([b_own, b_swapped], 1), jnp.concatenate([v_across, v_across_other], 1)
        ) + dott(
            jnp.concatenate([a01_own, a01_swapped], 1),
            jnp.concatenate([columns(value_next, 0, 2), columns(v_other, 0, 2)], 1),
        )
        own01 = adjoint_of(jnp.concatenate([a0, a1], 1), jnp.concatenate([a0_next, a1_next], 1))
        near, far = together((a23, a23_next), grad, own01)
        a23_own, a23_swapped = own_and_swapped(near, far)
        grad = df * (grad + dott(
            jnp.concatenate([a23_own, a23_swapped], 1),
            jnp.concatenate([columns(value_next, 2, 4), columns(v_other, 2, 4)], 1),
        ))
        own23 = adjoint_of(near, far)
        own23, part3, grad = together((own23, part3, grad))
        adjoint = df * (
            jnp.concatenate([own01, own23], 1) + jnp.concatenate([part0, part1, part2, part3], 1)
        )
        return adjoint, grad

    return shards


def solution(mesh):
    sizes = tuple(mesh.shape[a] for a in AXES)
    shards = two_side_shards(sizes) if sizes[1:] == (4, 2, 2) else plain_shards
    return jax.shard_map(
        shards,
        mesh=mesh,
        in_specs=(
            P(("groups", "markov"), ("storage", "sub")),
            P(("groups", "markov"), ("storage", "sub")),
            P(("groups", "storage", "sub"), "markov"),
            P("groups"),
        ),
        out_specs=(
            P(("groups", "markov"), ("storage", "sub")),
            P(("groups", "storage", "sub"), "markov"),
        ),
        check_vma=False,
    )
```

```python
import jax
import jax.numpy as jnp
from jax import lax
from jax.sharding import PartitionSpec as P

discount_rate = 0.97
AXES = ("groups", "markov", "storage", "sub")


def factor_of(section):
    return jnp.exp(section[0].astype(jnp.float32) * jnp.log(jnp.float32(discount_rate)))


def plain_shards(expected_cot, value_next, transition, section):
    discount_factor = factor_of(section)
    cotangent_all = lax.all_gather(expected_cot, "markov", axis=0, tiled=True)
    adjoint_sum = lax.dot_general(
        lax.all_gather(transition, ("storage", "sub"), axis=0, tiled=True),
        cotangent_all,
        (((0,), (0,)), ((), ())),
        preferred_element_type=jnp.float32,
    )
    own_states = lax.all_to_all(
        cotangent_all, ("storage", "sub"), split_axis=0, concat_axis=1, tiled=True
    )
    gathered_values = lax.all_gather(value_next, ("storage", "sub"), axis=1, tiled=True)
    gradient_sum = lax.dot_general(
        own_states, gathered_values, (((1,), (1,)), ((), ())), preferred_element_type=jnp.float32
    )
    return (discount_factor * adjoint_sum, discount_factor * gradient_sum)


def tdot(a, b):
    return lax.dot_general(a, b, (((0,), (0,)), ((), ())), preferred_element_type=jnp.float32)


def dott(a, b):
    return lax.dot_general(a, b, (((1,), (1,)), ((), ())), preferred_element_type=jnp.float32)


def after(array, *others):
    return lax.optimization_barrier((array,) + others)[0]


def two_side_shards(sizes):
    groups, layers, sides, cores = sizes
    places = [(g, z, s, c) for g in range(groups) for z in range(layers) for s in range(sides) for c in range(cores)]
    index = {place: i for i, place in enumerate(places)}

    def pairs(move, chosen=lambda g, z, s, c: True):
        return [(index[p], index[move(*p)]) for p in places if chosen(*p)]

    def is_home(g, z, s, c):
        return z // 2 == s

    def jumped(g, z, s, c):
        return (g, z ^ 2, s, c)

    cross_pairs = pairs(lambda g, z, s, c: (g, z, 1 - s, c))
    step_pairs = pairs(lambda g, z, s, c: (g, z ^ 1, s, c))
    core_pairs = pairs(lambda g, z, s, c: (g, z, s, 1 - c))
    jump_pairs, home_jump_pairs = pairs(jumped), pairs(jumped, is_home)

    def cross(a):
        return lax.ppermute(a, AXES, cross_pairs)

    def step(a):
        return lax.ppermute(a, AXES, step_pairs)

    def swap(a):
        return lax.ppermute(a, AXES, core_pairs)

    def home_jump(a):
        return lax.ppermute(a, AXES, home_jump_pairs)

    def jump(a):
        return lax.ppermute(a, AXES, jump_pairs)

    def shards(expected_cot, value_next, transition, section):
        df = factor_of(section)
        z, s, c = lax.axis_index("markov"), lax.axis_index("storage"), lax.axis_index("sub")
        home = z // 2 == s
        mine = z % 2 == c
        half = expected_cot.shape[1] // 2
        quarter = half // 2

        def columns(array, start, stop):
            return array[:, start * quarter : stop * quarter]

        def together(arrays, *gates):
            return lax.optimization_barrier(tuple(arrays) + gates)[: len(arrays)]

        e = [columns(expected_cot, i, i + 1) for i in range(4)]
        v = [columns(value_next, i, i + 1) for i in range(4)]
        x1 = cross(jnp.where(home, v[0], e[0]))
        t_other = swap(transition)
        e2 = after(e[2], x1)
        j1 = jump(jnp.where(home, x1, e2))
        v1, e1 = together((v[1], e[1]), x1)
        x2 = cross(jnp.concatenate([jnp.where(home, v1, e1), v[2]], 1))
        x2, v_across2 = columns(x2, 0, 1), columns(x2, 1, 2)
        t, t_o = together((transition, t_other), x1)
        t_near, t_next = jnp.where(mine, t, t_o), jnp.where(mine, t_o, t)

        def adjoint_of(near, far):
            return tdot(t_near, near) + tdot(t_next, far)

        near, far = together((x1, j1), x2)
        b0 = jnp.where(home, near, far)
        b0_next = step(b0)
        near, far = together((x2, e[3]))
        j2 = jump(jnp.where(home, near, far))
        near, far = together((j1, v[0]), x2, t_near)
        x3 = cross(jnp.where(home, near, far))
        sum0 = adjoint_of(b0, b0_next)
        near, far = together((e[0], x3))
        third = jnp.where(home, near, far)
        j3 = jump(third)
        near, far = together((x2, j2), sum0, third)
        b1 = jnp.where(home, near, far)
        b1_next = step(b1)
        near, far = together((j2, v[1]), third, sum0)
        x4 = cross(jnp.where(home, near, far))
        part0 = cross(after(sum0, x4))
        near, far = together((e[1], x4))
        j4 = jump(jnp.where(home, near, far))
        sum1 = adjoint_of(b1, b1_next)
        part1 = cross(after(sum1, part0))
        v_across3 = cross(after(v[3], part0))
        near, both, far = together((e[0], j3, x3), sum1, x4)
        a0b2 = jnp.where(home, jnp.concatenate([near, both], 1), jnp.concatenate([both, far], 1))
        a0b2_next = step(a0b2)
        sum2 = adjoint_of(columns(a0b2, 1, 2), columns(a0b2_next, 1, 2))
        part2 = cross(after(sum2, part1))
        j5 = home_jump(after(columns(expected_cot, 2, 4), j3))
        near, both, far = together((e[1], j4, x4), sum2, part0)
        a1b3 = jnp.where(home, jnp.concatenate([near, both], 1), jnp.concatenate([both, far], 1))
        a1b3_next = step(a1b3)
        v_other = swap(after(value_next, sum1))
        sum3 = adjoint_of(columns(a1b3, 1, 2), columns(a1b3_next, 1, 2))
        part3 = cross(after(sum3, part2))

        def own_and_swapped(near, far):
            return jnp.where(mine, near, far), swap(jnp.where(mine, far, near))

        parts = together((x1, x2, x3, x4, v_across2, v_across3), sum1)
        v_across = jnp.concatenate(
            [jnp.where(home, parts[2], parts[0]), jnp.where(home, parts[3], parts[1]), parts[4], parts[5]], 1
        )
        v_across_other = swap(v_across)
        near, far = together((columns(expected_cot, 2, 4), j5), a1b3_next, part2)
        a23 = jnp.where(home, near, far)
        a23_next = step(a23)
        b0, b0_next, b1, b1_next, a0b2, a0b2_next = together(
            (b0, b0_next, b1, b1_next, a0b2, a0b2_next), a1b3_next, sum3, part2
        )
        a0, a0_next = columns(a0b2, 0, 1), columns(a0b2_next, 0, 1)
        a1, a1_next = columns(a1b3, 0, 1), columns(a1b3_next, 0, 1)
        b_own, b_swapped = own_and_swapped(
            jnp.concatenate([b0, b1, columns(a0b2, 1, 2), columns(a1b3, 1, 2)], 1),
            jnp.concatenate([b0_next, b1_next, columns(a0b2_next, 1, 2), columns(a1b3_next, 1, 2)], 1),
        )
        a01_own, a01_swapped = own_and_swapped(
            jnp.concatenate([a0, a1], 1), jnp.concatenate([a0_next, a1_next], 1)
        )
        grad = dott(
            jnp.concatenate([b_own, b_swapped], 1), jnp.concatenate([v_across, v_across_other], 1)
        ) + dott(
            jnp.concatenate([a01_own, a01_swapped], 1),
            jnp.concatenate([columns(value_next, 0, 2), columns(v_other, 0, 2)], 1),
        )
        own01 = adjoint_of(jnp.concatenate([a0, a1], 1), jnp.concatenate([a0_next, a1_next], 1))
        near, far = together((a23, a23_next), grad, own01)
        a23_own, a23_swapped = own_and_swapped(near, far)
        grad = df * (grad + dott(
            jnp.concatenate([a23_own, a23_swapped], 1),
            jnp.concatenate([columns(value_next, 2, 4), columns(v_other, 2, 4)], 1),
        ))
        own23 = adjoint_of(near, far)
        own23, part3, grad = together((own23, part3, grad))
        adjoint = df * (
            jnp.concatenate([own01, own23], 1) + jnp.concatenate([part0, part1, part2, part3], 1)
        )
        return adjoint, grad

    return shards


def solution(mesh):
    sizes = tuple(mesh.shape[a] for a in AXES)
    shards = two_side_shards(sizes) if sizes[1:] == (4, 2, 2) else plain_shards
    return jax.shard_map(
        shards,
        mesh=mesh,
        in_specs=(
            P(("groups", "markov"), ("storage", "sub")),
            P(("groups", "markov"), ("storage", "sub")),
            P(("groups", "storage", "sub"), "markov"),
            P("groups"),
        ),
        out_specs=(
            P(("groups", "markov"), ("storage", "sub")),
            P(("groups", "storage", "sub"), "markov"),
        ),
        check_vma=False,
    )
```

```python
import jax
import jax.numpy as jnp
from jax import lax
from jax.sharding import PartitionSpec as P

discount_rate = 0.97
AXES = ("groups", "markov", "storage", "sub")


def factor_of(section):
    return jnp.exp(section[0].astype(jnp.float32) * jnp.log(jnp.float32(discount_rate)))


def plain_shards(expected_cot, value_next, transition, section):
    discount_factor = factor_of(section)
    cotangent_all = lax.all_gather(expected_cot, "markov", axis=0, tiled=True)
    adjoint_sum = lax.dot_general(
        lax.all_gather(transition, ("storage", "sub"), axis=0, tiled=True),
        cotangent_all,
        (((0,), (0,)), ((), ())),
        preferred_element_type=jnp.float32,
    )
    own_states = lax.all_to_all(
        cotangent_all, ("storage", "sub"), split_axis=0, concat_axis=1, tiled=True
    )
    gathered_values = lax.all_gather(value_next, ("storage", "sub"), axis=1, tiled=True)
    gradient_sum = lax.dot_general(
        own_states, gathered_values, (((1,), (1,)), ((), ())), preferred_element_type=jnp.float32
    )
    return (discount_factor * adjoint_sum, discount_factor * gradient_sum)


def tdot(a, b):
    return lax.dot_general(a, b, (((0,), (0,)), ((), ())), preferred_element_type=jnp.float32)


def dott(a, b):
    return lax.dot_general(a, b, (((1,), (1,)), ((), ())), preferred_element_type=jnp.float32)


def after(array, *others):
    return lax.optimization_barrier((array,) + others)[0]


def two_side_shards(sizes):
    groups, layers, sides, cores = sizes
    places = [(g, z, s, c) for g in range(groups) for z in range(layers) for s in range(sides) for c in range(cores)]
    index = {place: i for i, place in enumerate(places)}

    def pairs(move, chosen=lambda g, z, s, c: True):
        return [(index[p], index[move(*p)]) for p in places if chosen(*p)]

    def is_home(g, z, s, c):
        return z // 2 == s

    def jumped(g, z, s, c):
        return (g, z ^ 2, s, c)

    cross_pairs = pairs(lambda g, z, s, c: (g, z, 1 - s, c))
    step_pairs = pairs(lambda g, z, s, c: (g, z ^ 1, s, c))
    core_pairs = pairs(lambda g, z, s, c: (g, z, s, 1 - c))
    jump_pairs, home_jump_pairs = pairs(jumped), pairs(jumped, is_home)

    def cross(a):
        return lax.ppermute(a, AXES, cross_pairs)

    def step(a):
        return lax.ppermute(a, AXES, step_pairs)

    def swap(a):
        return lax.ppermute(a, AXES, core_pairs)

    def home_jump(a):
        return lax.ppermute(a, AXES, home_jump_pairs)

    def jump(a):
        return lax.ppermute(a, AXES, jump_pairs)

    def shards(expected_cot, value_next, transition, section):
        df = factor_of(section)
        z, s, c = lax.axis_index("markov"), lax.axis_index("storage"), lax.axis_index("sub")
        home = z // 2 == s
        mine = z % 2 == c
        half = expected_cot.shape[1] // 2
        quarter = half // 2

        def columns(array, start, stop):
            return array[:, start * quarter : stop * quarter]

        def together(arrays, *gates):
            return lax.optimization_barrier(tuple(arrays) + gates)[: len(arrays)]

        e = [columns(expected_cot, i, i + 1) for i in range(4)]
        v = [columns(value_next, i, i + 1) for i in range(4)]
        x1 = cross(jnp.where(home, v[0], e[0]))
        t_other = swap(transition)
        e2 = after(e[2], x1)
        j1 = jump(jnp.where(home, x1, e2))
        v1, e1 = together((v[1], e[1]), x1)
        x2 = cross(jnp.concatenate([jnp.where(home, v1, e1), v[2]], 1))
        x2, v_across2 = columns(x2, 0, 1), columns(x2, 1, 2)
        t, t_o = together((transition, t_other), x1)
        t_near, t_next = jnp.where(mine, t, t_o), jnp.where(mine, t_o, t)

        def adjoint_of(near, far):
            return tdot(t_near, near) + tdot(t_next, far)

        near, far = together((x1, j1), x2)
        b0 = jnp.where(home, near, far)
        b0_next = step(b0)
        near, far = together((x2, e[3]))
        j2 = jump(jnp.where(home, near, far))
        near, far = together((j1, v[0]), x2, t_near)
        x3 = cross(jnp.where(home, near, far))
        sum0 = adjoint_of(b0, b0_next)
        part0 = cross(after(sum0, x3))
        near, far = together((e[0], x3))
        third = jnp.where(home, near, far)
        j3 = jump(third)
        near, far = together((x2, j2), sum0, third)
        b1 = jnp.where(home, near, far)
        b1_next = step(b1)
        near, far = together((j2, v[1]), third, sum0)
        x4 = cross(jnp.where(home, near, far))
        near, far = together((e[1], x4))
        j4 = jump(jnp.where(home, near, far))
        sum1 = adjoint_of(b1, b1_next)
        part1 = cross(after(sum1, part0))
        v_across3 = cross(after(v[3], part1))
        near, both, far = together((e[0], j3, x3), sum1, x4, part0)
        a0b2 = jnp.where(home, jnp.concatenate([near, both], 1), jnp.concatenate([both, far], 1))
        a0b2_next = step(a0b2)
        sum2 = adjoint_of(columns(a0b2, 1, 2), columns(a0b2_next, 1, 2))
        part2 = cross(after(sum2, part1))
        j5 = home_jump(after(columns(expected_cot, 2, 4), j3))
        near, both, far = together((e[1], j4, x4), sum2)
        a1b3 = jnp.where(home, jnp.concatenate([near, both], 1), jnp.concatenate([both, far], 1))
        a1b3_next = step(a1b3)
        v_other = swap(after(value_next, sum1))
        sum3 = adjoint_of(columns(a1b3, 1, 2), columns(a1b3_next, 1, 2))
        part3 = cross(after(sum3, part2))

        def own_and_swapped(near, far):
            return jnp.where(mine, near, far), swap(jnp.where(mine, far, near))

        parts = together((x1, x2, x3, x4, v_across2, v_across3), sum1)
        v_across = jnp.concatenate(
            [jnp.where(home, parts[2], parts[0]), jnp.where(home, parts[3], parts[1]), parts[4], parts[5]], 1
        )
        v_across_other = swap(v_across)
        near, far = together((columns(expected_cot, 2, 4), j5), a1b3_next, part1)
        a23 = jnp.where(home, near, far)
        a23_next = step(a23)
        b0, b0_next, b1, b1_next, a0b2, a0b2_next = together(
            (b0, b0_next, b1, b1_next, a0b2, a0b2_next), a1b3_next, sum3, part2, a23
        )
        a0, a0_next = columns(a0b2, 0, 1), columns(a0b2_next, 0, 1)
        a1, a1_next = columns(a1b3, 0, 1), columns(a1b3_next, 0, 1)
        b_own, b_swapped = own_and_swapped(
            jnp.concatenate([b0, b1, columns(a0b2, 1, 2), columns(a1b3, 1, 2)], 1),
            jnp.concatenate([b0_next, b1_next, columns(a0b2_next, 1, 2), columns(a1b3_next, 1, 2)], 1),
        )
        a01_own, a01_swapped = own_and_swapped(
            jnp.concatenate([a0, a1], 1), jnp.concatenate([a0_next, a1_next], 1)
        )
        grad = dott(
            jnp.concatenate([b_own, b_swapped], 1), jnp.concatenate([v_across, v_across_other], 1)
        ) + dott(
            jnp.concatenate([a01_own, a01_swapped], 1),
            jnp.concatenate([columns(value_next, 0, 2), columns(v_other, 0, 2)], 1),
        )
        own01 = adjoint_of(jnp.concatenate([a0, a1], 1), jnp.concatenate([a0_next, a1_next], 1))
        near, far = together((a23, a23_next), grad, own01)
        a23_own, a23_swapped = own_and_swapped(near, far)
        grad = df * (grad + dott(
            jnp.concatenate([a23_own, a23_swapped], 1),
            jnp.concatenate([columns(value_next, 2, 4), columns(v_other, 2, 4)], 1),
        ))
        own23 = adjoint_of(near, far)
        own23, part3, grad = together((own23, part3, grad))
        adjoint = df * (
            jnp.concatenate([own01, own23], 1) + jnp.concatenate([part0, part1, part2, part3], 1)
        )
        return adjoint, grad

    return shards


def solution(mesh):
    sizes = tuple(mesh.shape[a] for a in AXES)
    shards = two_side_shards(sizes) if sizes[1:] == (4, 2, 2) else plain_shards
    return jax.shard_map(
        shards,
        mesh=mesh,
        in_specs=(
            P(("groups", "markov"), ("storage", "sub")),
            P(("groups", "markov"), ("storage", "sub")),
            P(("groups", "storage", "sub"), "markov"),
            P("groups"),
        ),
        out_specs=(
            P(("groups", "markov"), ("storage", "sub")),
            P(("groups", "storage", "sub"), "markov"),
        ),
        check_vma=False,
    )
```

```python
import jax
import jax.numpy as jnp
from jax import lax
from jax.sharding import PartitionSpec as P

discount_rate = 0.97
AXES = ("groups", "markov", "storage", "sub")


def factor_of(section):
    return jnp.exp(section[0].astype(jnp.float32) * jnp.log(jnp.float32(discount_rate)))


def plain_shards(expected_cot, value_next, transition, section):
    discount_factor = factor_of(section)
    cotangent_all = lax.all_gather(expected_cot, "markov", axis=0, tiled=True)
    adjoint_sum = lax.dot_general(
        lax.all_gather(transition, ("storage", "sub"), axis=0, tiled=True),
        cotangent_all,
        (((0,), (0,)), ((), ())),
        preferred_element_type=jnp.float32,
    )
    own_states = lax.all_to_all(
        cotangent_all, ("storage", "sub"), split_axis=0, concat_axis=1, tiled=True
    )
    gathered_values = lax.all_gather(value_next, ("storage", "sub"), axis=1, tiled=True)
    gradient_sum = lax.dot_general(
        own_states, gathered_values, (((1,), (1,)), ((), ())), preferred_element_type=jnp.float32
    )
    return (discount_factor * adjoint_sum, discount_factor * gradient_sum)


def tdot(a, b):
    return lax.dot_general(a, b, (((0,), (0,)), ((), ())), preferred_element_type=jnp.float32)


def dott(a, b):
    return lax.dot_general(a, b, (((1,), (1,)), ((), ())), preferred_element_type=jnp.float32)


def after(array, *others):
    return lax.optimization_barrier((array,) + others)[0]


def two_side_shards(sizes):
    groups, layers, sides, cores = sizes
    places = [(g, z, s, c) for g in range(groups) for z in range(layers) for s in range(sides) for c in range(cores)]
    index = {place: i for i, place in enumerate(places)}

    def pairs(move, chosen=lambda g, z, s, c: True):
        return [(index[p], index[move(*p)]) for p in places if chosen(*p)]

    def is_home(g, z, s, c):
        return z // 2 == s

    def jumped(g, z, s, c):
        return (g, z ^ 2, s, c)

    cross_pairs = pairs(lambda g, z, s, c: (g, z, 1 - s, c))
    step_pairs = pairs(lambda g, z, s, c: (g, z ^ 1, s, c))
    core_pairs = pairs(lambda g, z, s, c: (g, z, s, 1 - c))
    jump_pairs, home_jump_pairs = pairs(jumped), pairs(jumped, is_home)

    def cross(a):
        return lax.ppermute(a, AXES, cross_pairs)

    def step(a):
        return lax.ppermute(a, AXES, step_pairs)

    def swap(a):
        return lax.ppermute(a, AXES, core_pairs)

    def home_jump(a):
        return lax.ppermute(a, AXES, home_jump_pairs)

    def jump(a):
        return lax.ppermute(a, AXES, jump_pairs)

    def shards(expected_cot, value_next, transition, section):
        df = factor_of(section)
        z, s, c = lax.axis_index("markov"), lax.axis_index("storage"), lax.axis_index("sub")
        home = z // 2 == s
        mine = z % 2 == c
        half = expected_cot.shape[1] // 2
        quarter = half // 2

        def columns(array, start, stop):
            return array[:, start * quarter : stop * quarter]

        def together(arrays, *gates):
            return lax.optimization_barrier(tuple(arrays) + gates)[: len(arrays)]

        e = [columns(expected_cot, i, i + 1) for i in range(4)]
        v = [columns(value_next, i, i + 1) for i in range(4)]
        x1 = cross(jnp.where(home, v[0], e[0]))
        t_other = swap(transition)
        e2 = after(e[2], x1)
        j1 = jump(jnp.where(home, x1, e2))
        t_near, t_next = jnp.where(mine, transition, t_other), jnp.where(mine, t_other, transition)

        def adjoint_of(near, far):
            return tdot(t_near, near) + tdot(t_next, far)

        v1, e1 = together((v[1], e[1]), x1, t_near)
        x2 = cross(jnp.concatenate([jnp.where(home, v1, e1), v[2], v[3]], 1))
        x2, v_across2, v_across3 = columns(x2, 0, 1), columns(x2, 1, 2), columns(x2, 2, 3)
        second = jnp.where(home, x2, e[3])
        j2 = jump(second)
        near, far = together((j1, v[0]), second)
        third_cross = jnp.where(home, near, far)
        x3 = cross(third_cross)
        near, far = together((x1, j1), third_cross)
        b0 = jnp.where(home, near, far)
        b0_next = step(b0)
        third = jnp.where(home, e[0], x3)
        j3 = jump(third)
        sum0 = adjoint_of(b0, b0_next)
        near, far = together((j2, v[1]), third)
        x4 = cross(jnp.where(home, near, far))
        near, far = together((x2, j2), sum0, third)
        b1 = jnp.where(home, near, far)
        b1_next = step(b1)
        part0 = cross(after(sum0, x4))
        fourth = jnp.where(home, e[1], x4)
        j4 = jump(fourth)
        sum1 = adjoint_of(b1, b1_next)
        part1 = cross(after(sum1, part0))
        near, both, far = together((e[0], j3, x3), sum1, fourth)
        a0b2 = jnp.where(home, jnp.concatenate([near, both], 1), jnp.concatenate([both, far], 1))
        a0b2_next = step(a0b2)
        sum2 = adjoint_of(columns(a0b2, 1, 2), columns(a0b2_next, 1, 2))
        part2 = cross(after(sum2, part1))
        j5 = home_jump(after(columns(expected_cot, 2, 4), j3))
        near, both, far = together((e[1], j4, x4), sum2, part0)
        a1b3 = jnp.where(home, jnp.concatenate([near, both], 1), jnp.concatenate([both, far], 1))
        a1b3_next = step(a1b3)
        v_other = swap(after(value_next, sum1))
        sum3 = adjoint_of(columns(a1b3, 1, 2), columns(a1b3_next, 1, 2))
        part3 = cross(after(sum3, part2))

        def own_and_swapped(near, far):
            return jnp.where(mine, near, far), swap(jnp.where(mine, far, near))

        parts = together((x1, x2, x3, x4, v_across2, v_across3), sum1)
        v_across = jnp.concatenate(
            [jnp.where(home, parts[2], parts[0]), jnp.where(home, parts[3], parts[1]), parts[4], parts[5]], 1
        )
        v_across_other = swap(v_across)
        near, far = together((columns(expected_cot, 2, 4), j5), a1b3_next, part1)
        a23 = jnp.where(home, near, far)
        a23_next = step(a23)
        b0, b0_next, b1, b1_next, a0b2, a0b2_next = together(
            (b0, b0_next, b1, b1_next, a0b2, a0b2_next), a1b3_next, sum3, part2, a23
        )
        a0, a0_next = columns(a0b2, 0, 1), columns(a0b2_next, 0, 1)
        a1, a1_next = columns(a1b3, 0, 1), columns(a1b3_next, 0, 1)
        b_own, b_swapped = own_and_swapped(
            jnp.concatenate([b0, b1, columns(a0b2, 1, 2), columns(a1b3, 1, 2)], 1),
            jnp.concatenate([b0_next, b1_next, columns(a0b2_next, 1, 2), columns(a1b3_next, 1, 2)], 1),
        )
        a01_own, a01_swapped = own_and_swapped(
            jnp.concatenate([a0, a1], 1), jnp.concatenate([a0_next, a1_next], 1)
        )
        grad = dott(
            jnp.concatenate([b_own, b_swapped], 1), jnp.concatenate([v_across, v_across_other], 1)
        ) + dott(
            jnp.concatenate([a01_own, a01_swapped], 1),
            jnp.concatenate([columns(value_next, 0, 2), columns(v_other, 0, 2)], 1),
        )
        own01 = adjoint_of(jnp.concatenate([a0, a1], 1), jnp.concatenate([a0_next, a1_next], 1))
        near, far = together((a23, a23_next), grad, own01)
        a23_own, a23_swapped = own_and_swapped(near, far)
        grad = df * (grad + dott(
            jnp.concatenate([a23_own, a23_swapped], 1),
            jnp.concatenate([columns(value_next, 2, 4), columns(v_other, 2, 4)], 1),
        ))
        own23 = adjoint_of(near, far)
        own23, part3, grad = together((own23, part3, grad))
        adjoint = df * (
            jnp.concatenate([own01, own23], 1) + jnp.concatenate([part0, part1, part2, part3], 1)
        )
        return adjoint, grad

    return shards


def solution(mesh):
    sizes = tuple(mesh.shape[a] for a in AXES)
    shards = two_side_shards(sizes) if sizes[1:] == (4, 2, 2) else plain_shards
    return jax.shard_map(
        shards,
        mesh=mesh,
        in_specs=(
            P(("groups", "markov"), ("storage", "sub")),
            P(("groups", "markov"), ("storage", "sub")),
            P(("groups", "storage", "sub"), "markov"),
            P("groups"),
        ),
        out_specs=(
            P(("groups", "markov"), ("storage", "sub")),
            P(("groups", "storage", "sub"), "markov"),
        ),
        check_vma=False,
    )
```

```python
import jax
import jax.numpy as jnp
from jax import lax
from jax.sharding import PartitionSpec as P

discount_rate = 0.97
AXES = ("groups", "markov", "storage", "sub")


def factor_of(section):
    return jnp.exp(section[0].astype(jnp.float32) * jnp.log(jnp.float32(discount_rate)))


def plain_shards(expected_cot, value_next, transition, section):
    discount_factor = factor_of(section)
    cotangent_all = lax.all_gather(expected_cot, "markov", axis=0, tiled=True)
    adjoint_sum = lax.dot_general(
        lax.all_gather(transition, ("storage", "sub"), axis=0, tiled=True),
        cotangent_all,
        (((0,), (0,)), ((), ())),
        preferred_element_type=jnp.float32,
    )
    own_states = lax.all_to_all(
        cotangent_all, ("storage", "sub"), split_axis=0, concat_axis=1, tiled=True
    )
    gathered_values = lax.all_gather(value_next, ("storage", "sub"), axis=1, tiled=True)
    gradient_sum = lax.dot_general(
        own_states, gathered_values, (((1,), (1,)), ((), ())), preferred_element_type=jnp.float32
    )
    return (discount_factor * adjoint_sum, discount_factor * gradient_sum)


def tdot(a, b):
    return lax.dot_general(a, b, (((0,), (0,)), ((), ())), preferred_element_type=jnp.float32)


def dott(a, b):
    return lax.dot_general(a, b, (((1,), (1,)), ((), ())), preferred_element_type=jnp.float32)


def after(array, *others):
    return lax.optimization_barrier((array,) + others)[0]


def two_side_shards(sizes):
    groups, layers, sides, cores = sizes
    places = [(g, z, s, c) for g in range(groups) for z in range(layers) for s in range(sides) for c in range(cores)]
    index = {place: i for i, place in enumerate(places)}

    def pairs(move, chosen=lambda g, z, s, c: True):
        return [(index[p], index[move(*p)]) for p in places if chosen(*p)]

    def is_home(g, z, s, c):
        return z // 2 == s

    def jumped(g, z, s, c):
        return (g, z ^ 2, s, c)

    cross_pairs = pairs(lambda g, z, s, c: (g, z, 1 - s, c))
    step_pairs = pairs(lambda g, z, s, c: (g, z ^ 1, s, c))
    core_pairs = pairs(lambda g, z, s, c: (g, z, s, 1 - c))
    jump_pairs, home_jump_pairs = pairs(jumped), pairs(jumped, is_home)

    def cross(a):
        return lax.ppermute(a, AXES, cross_pairs)

    def step(a):
        return lax.ppermute(a, AXES, step_pairs)

    def swap(a):
        return lax.ppermute(a, AXES, core_pairs)

    def home_jump(a):
        return lax.ppermute(a, AXES, home_jump_pairs)

    def jump(a):
        return lax.ppermute(a, AXES, jump_pairs)

    def shards(expected_cot, value_next, transition, section):
        df = factor_of(section)
        z, s, c = lax.axis_index("markov"), lax.axis_index("storage"), lax.axis_index("sub")
        home = z // 2 == s
        mine = z % 2 == c
        half = expected_cot.shape[1] // 2
        quarter = half // 2

        def columns(array, start, stop):
            return array[:, start * quarter : stop * quarter]

        def together(arrays, *gates):
            return lax.optimization_barrier(tuple(arrays) + gates)[: len(arrays)]

        e = [columns(expected_cot, i, i + 1) for i in range(4)]
        v = [columns(value_next, i, i + 1) for i in range(4)]
        x1 = cross(jnp.where(home, v[0], e[0]))
        j0 = home_jump(e[0])
        t_other = swap(transition)
        t_near, t_next = jnp.where(mine, transition, t_other), jnp.where(mine, t_other, transition)

        def adjoint_of(near, far):
            return tdot(t_near, near) + tdot(t_next, far)

        v1, e1 = together((v[1], e[1]), x1, t_near, j0)
        x2 = cross(jnp.concatenate([jnp.where(home, v1, e1), v[2]], 1))
        x2, v_across2 = columns(x2, 0, 1), columns(x2, 1, 2)
        near, far = together((x1, e[2]), j0)
        j1 = jump(jnp.where(home, near, far))
        near, far = together((e[0], j0), x1)
        a0 = jnp.where(home, near, far)
        a0_next = step(a0)
        near, far = together((x2, e[3]), j1)
        second = jnp.where(home, near, far)
        j2 = jump(second)
        near, far = together((j1, v[0]), second, a0_next)
        third_cross = jnp.where(home, near, far)
        x3 = cross(jnp.concatenate([third_cross, v[3]], 1))
        x3, v_across3 = columns(x3, 0, 1), columns(x3, 1, 2)
        near, far = together((x1, j1), third_cross)
        b0 = jnp.where(home, near, far)
        b0_next = step(b0)
        third = jnp.where(home, e[1], x3)
        j3 = jump(third)
        sum0 = adjoint_of(b0, b0_next)
        near, far = together((j2, v[1]), third)
        x4 = cross(jnp.where(home, near, far))
        near, far = together((x2, j2), sum0, third)
        b1 = jnp.where(home, near, far)
        b1_next = step(b1)
        part0 = cross(after(sum0, x4))
        fourth = jnp.where(home, e[2], x4)
        j4 = jump(fourth)
        sum1 = adjoint_of(b1, after(b1_next, part0))
        part1 = cross(sum1)
        near, both, far = together((e[1], j3, x3), b1_next, fourth)
        a1b2 = jnp.where(home, jnp.concatenate([near, both], 1), jnp.concatenate([both, far], 1))
        a1b2_next = step(a1b2)
        sum2 = adjoint_of(columns(a1b2, 1, 2), columns(after(a1b2_next, part1), 1, 2))
        part2 = cross(sum2)
        j5 = home_jump(after(e[3], j3))
        near, both, far = together((e[2], j4, x4), a1b2_next, part0)
        a2b3 = jnp.where(home, jnp.concatenate([near, both], 1), jnp.concatenate([both, far], 1))
        a2b3_next = step(a2b3)
        v_other = swap(after(value_next, b1_next))
        sum3 = adjoint_of(columns(a2b3, 1, 2), columns(after(a2b3_next, part2), 1, 2))
        part3 = cross(sum3)

        def product(near, far, values, values_other):
            own, swapped = jnp.where(mine, near, far), swap(jnp.where(mine, far, near))
            return dott(jnp.concatenate([own, swapped], 1), jnp.concatenate(values + values_other, 1))

        parts = together((x1, x2, x3, x4, v_across2, v_across3), b1_next)
        v_across = jnp.concatenate(
            [jnp.where(home, parts[2], parts[0]), jnp.where(home, parts[3], parts[1]), parts[4], parts[5]], 1
        )
        v_across_other = swap(v_across)
        w, w_other, u, u_other = (
            [columns(array, i, i + 1) for i in range(4)] for array in (value_next, v_other, v_across, v_across_other)
        )
        early = together((b0, b1, a1b2, a0, b0_next, b1_next, a1b2_next, a0_next), a2b3, sum2)
        grad = product(
            jnp.concatenate(early[:4], 1),
            jnp.concatenate(early[4:], 1),
            [u[0], u[1], w[1], u[2], w[0]],
            [u_other[0], u_other[1], w_other[1], u_other[2], w_other[0]],
        )
        near, far = together((e[3], j5), a2b3_next, part1, grad)
        a3 = jnp.where(home, near, far)
        a3_next = step(a3)
        near, far = together((a2b3, a2b3_next), a3, sum3)
        grad = grad + product(near, far, [w[2], u[3]], [w_other[2], u_other[3]])
        a1, a1_next = columns(a1b2, 0, 1), columns(a1b2_next, 0, 1)
        own012 = adjoint_of(
            jnp.concatenate([a0, a1, columns(near, 0, 1)], 1),
            jnp.concatenate([a0_next, a1_next, columns(far, 0, 1)], 1),
        )
        near, far = together((a3, a3_next), grad, own012)
        grad = df * (grad + product(near, far, [w[3]], [w_other[3]]))
        own3 = adjoint_of(near, far)
        own3, part3, grad = together((own3, part3, grad))
        adjoint = df * (
            jnp.concatenate([own012, own3], 1) + jnp.concatenate([part0, part1, part2, part3], 1)
        )
        return adjoint, grad

    return shards


def solution(mesh):
    sizes = tuple(mesh.shape[a] for a in AXES)
    shards = two_side_shards(sizes) if sizes[1:] == (4, 2, 2) else plain_shards
    return jax.shard_map(
        shards,
        mesh=mesh,
        in_specs=(
            P(("groups", "markov"), ("storage", "sub")),
            P(("groups", "markov"), ("storage", "sub")),
            P(("groups", "storage", "sub"), "markov"),
            P("groups"),
        ),
        out_specs=(
            P(("groups", "markov"), ("storage", "sub")),
            P(("groups", "storage", "sub"), "markov"),
        ),
        check_vma=False,
    )
```

```python
import jax
import jax.numpy as jnp
from jax import lax
from jax.sharding import PartitionSpec as P

discount_rate = 0.97
AXES = ("groups", "markov", "storage", "sub")


def factor_of(section):
    return jnp.exp(section[0].astype(jnp.float32) * jnp.log(jnp.float32(discount_rate)))


def plain_shards(expected_cot, value_next, transition, section):
    discount_factor = factor_of(section)
    cotangent_all = lax.all_gather(expected_cot, "markov", axis=0, tiled=True)
    adjoint_sum = lax.dot_general(
        lax.all_gather(transition, ("storage", "sub"), axis=0, tiled=True),
        cotangent_all,
        (((0,), (0,)), ((), ())),
        preferred_element_type=jnp.float32,
    )
    own_states = lax.all_to_all(
        cotangent_all, ("storage", "sub"), split_axis=0, concat_axis=1, tiled=True
    )
    gathered_values = lax.all_gather(value_next, ("storage", "sub"), axis=1, tiled=True)
    gradient_sum = lax.dot_general(
        own_states, gathered_values, (((1,), (1,)), ((), ())), preferred_element_type=jnp.float32
    )
    return (discount_factor * adjoint_sum, discount_factor * gradient_sum)


def tdot(a, b):
    return lax.dot_general(a, b, (((0,), (0,)), ((), ())), preferred_element_type=jnp.float32)


def dott(a, b):
    return lax.dot_general(a, b, (((1,), (1,)), ((), ())), preferred_element_type=jnp.float32)


def after(array, *others):
    return lax.optimization_barrier((array,) + others)[0]


def two_side_shards(sizes):
    groups, layers, sides, cores = sizes
    places = [(g, z, s, c) for g in range(groups) for z in range(layers) for s in range(sides) for c in range(cores)]
    index = {place: i for i, place in enumerate(places)}

    def pairs(move, chosen=lambda g, z, s, c: True):
        return [(index[p], index[move(*p)]) for p in places if chosen(*p)]

    def is_home(g, z, s, c):
        return z // 2 == s

    def jumped(g, z, s, c):
        return (g, z ^ 2, s, c)

    cross_pairs = pairs(lambda g, z, s, c: (g, z, 1 - s, c))
    step_pairs = pairs(lambda g, z, s, c: (g, z ^ 1, s, c))
    core_pairs = pairs(lambda g, z, s, c: (g, z, s, 1 - c))
    jump_pairs, home_jump_pairs = pairs(jumped), pairs(jumped, is_home)

    def cross(a):
        return lax.ppermute(a, AXES, cross_pairs)

    def step(a):
        return lax.ppermute(a, AXES, step_pairs)

    def swap(a):
        return lax.ppermute(a, AXES, core_pairs)

    def home_jump(a):
        return lax.ppermute(a, AXES, home_jump_pairs)

    def jump(a):
        return lax.ppermute(a, AXES, jump_pairs)

    def shards(expected_cot, value_next, transition, section):
        df = factor_of(section)
        z, s, c = lax.axis_index("markov"), lax.axis_index("storage"), lax.axis_index("sub")
        home = z // 2 == s
        mine = z % 2 == c
        half = expected_cot.shape[1] // 2
        quarter = half // 2

        def columns(array, start, stop):
            return array[:, start * quarter : stop * quarter]

        def together(arrays, *gates):
            return lax.optimization_barrier(tuple(arrays) + gates)[: len(arrays)]

        e = [columns(expected_cot, i, i + 1) for i in range(4)]
        v = [columns(value_next, i, i + 1) for i in range(4)]
        x1 = cross(jnp.where(home, v[0], e[0]))
        t_other = swap(transition)
        e2 = after(e[2], x1)
        j1 = jump(jnp.where(home, x1, e2))
        t_near, t_next = jnp.where(mine, transition, t_other), jnp.where(mine, t_other, transition)

        def adjoint_of(near, far):
            return tdot(t_near, near) + tdot(t_next, far)

        v1, e1 = together((v[1], e[1]), x1, t_near)
        x2 = cross(jnp.concatenate([jnp.where(home, v1, e1), v[2]], 1))
        x2, v_across2 = columns(x2, 0, 1), columns(x2, 1, 2)
        second = jnp.where(home, x2, e[3])
        j2 = jump(second)
        near, far = together((j1, v[0]), second)
        third_cross = jnp.where(home, near, far)
        x3 = cross(jnp.concatenate([third_cross, v[3]], 1))
        x3, v_across3 = columns(x3, 0, 1), columns(x3, 1, 2)
        near, far = together((x1, j1), third_cross)
        b0 = jnp.where(home, near, far)
        b0_next = step(b0)
        third = jnp.where(home, e[0], x3)
        j3 = jump(third)
        sum0 = adjoint_of(b0, b0_next)
        near, far = together((j2, v[1]), third)
        x4 = cross(jnp.where(home, near, far))
        near, far = together((x2, j2), sum0, third)
        b1 = jnp.where(home, near, far)
        b1_next = step(b1)
        part0 = cross(after(sum0, x4))
        fourth = jnp.where(home, e[1], x4)
        j4 = jump(fourth)
        sum1 = adjoint_of(b1, b1_next)
        part1 = cross(after(sum1, part0))
        near, both, far = together((e[0], j3, x3), sum1, fourth)
        a0b2 = jnp.where(home, jnp.concatenate([near, both], 1), jnp.concatenate([both, far], 1))
        a0b2_next = step(a0b2)
        sum2 = adjoint_of(columns(a0b2, 1, 2), columns(after(a0b2_next, part1), 1, 2))
        part2 = cross(sum2)
        j5 = home_jump(after(columns(expected_cot, 2, 4), j3))
        near, both, far = together((e[1], j4, x4), a0b2_next, part0)
        a1b3 = jnp.where(home, jnp.concatenate([near, both], 1), jnp.concatenate([both, far], 1))
        a1b3_next = step(a1b3)
        v_other = swap(after(value_next, sum1))
        sum3 = adjoint_of(columns(a1b3, 1, 2), columns(after(a1b3_next, part2), 1, 2))
        part3 = cross(sum3)

        def product(near, far, values, values_other):
            own, swapped = jnp.where(mine, near, far), swap(jnp.where(mine, far, near))
            return dott(jnp.concatenate([own, swapped], 1), jnp.concatenate(values + values_other, 1))

        parts = together((x1, x2, x3, x4, v_across2, v_across3), sum1)
        v_across = jnp.concatenate(
            [jnp.where(home, parts[2], parts[0]), jnp.where(home, parts[3], parts[1]), parts[4], parts[5]], 1
        )
        v_across_other = swap(v_across)
        w, w_other, u, u_other = (
            [columns(array, i, i + 1) for i in range(4)] for array in (value_next, v_other, v_across, v_across_other)
        )
        early = together((b0, b1, a0b2, b0_next, b1_next, a0b2_next), a1b3, sum2)
        grad = product(
            jnp.concatenate(early[:3], 1),
            jnp.concatenate(early[3:], 1),
            [u[0], u[1], w[0], u[2]],
            [u_other[0], u_other[1], w_other[0], u_other[2]],
        )
        near, far = together((columns(expected_cot, 2, 4), j5), a1b3_next, part1, grad)
        a23 = jnp.where(home, near, far)
        a23_next = step(a23)
        near, far = together((a1b3, a1b3_next), a23, sum3)
        grad = grad + product(near, far, [w[1], u[3]], [w_other[1], u_other[3]])
        own01 = adjoint_of(
            jnp.concatenate([columns(a0b2, 0, 1), columns(near, 0, 1)], 1),
            jnp.concatenate([columns(a0b2_next, 0, 1), columns(far, 0, 1)], 1),
        )
        near, far = together((a23, a23_next), grad, own01)
        grad = df * (grad + product(near, far, [w[2], w[3]], [w_other[2], w_other[3]]))
        own23 = adjoint_of(near, far)
        own23, part3, grad = together((own23, part3, grad))
        adjoint = df * (
            jnp.concatenate([own01, own23], 1) + jnp.concatenate([part0, part1, part2, part3], 1)
        )
        return adjoint, grad

    return shards


def solution(mesh):
    sizes = tuple(mesh.shape[a] for a in AXES)
    shards = two_side_shards(sizes) if sizes[1:] == (4, 2, 2) else plain_shards
    return jax.shard_map(
        shards,
        mesh=mesh,
        in_specs=(
            P(("groups", "markov"), ("storage", "sub")),
            P(("groups", "markov"), ("storage", "sub")),
            P(("groups", "storage", "sub"), "markov"),
            P("groups"),
        ),
        out_specs=(
            P(("groups", "markov"), ("storage", "sub")),
            P(("groups", "storage", "sub"), "markov"),
        ),
        check_vma=False,
    )
```

```python
import jax
import jax.numpy as jnp
from jax import lax
from jax.sharding import PartitionSpec as P

discount_rate = 0.97
AXES = ("groups", "markov", "storage", "sub")


def factor_of(section):
    return jnp.exp(section[0].astype(jnp.float32) * jnp.log(jnp.float32(discount_rate)))


def plain_shards(expected_cot, value_next, transition, section):
    discount_factor = factor_of(section)
    cotangent_all = lax.all_gather(expected_cot, "markov", axis=0, tiled=True)
    adjoint_sum = lax.dot_general(
        lax.all_gather(transition, ("storage", "sub"), axis=0, tiled=True),
        cotangent_all,
        (((0,), (0,)), ((), ())),
        preferred_element_type=jnp.float32,
    )
    own_states = lax.all_to_all(
        cotangent_all, ("storage", "sub"), split_axis=0, concat_axis=1, tiled=True
    )
    gathered_values = lax.all_gather(value_next, ("storage", "sub"), axis=1, tiled=True)
    gradient_sum = lax.dot_general(
        own_states, gathered_values, (((1,), (1,)), ((), ())), preferred_element_type=jnp.float32
    )
    return (discount_factor * adjoint_sum, discount_factor * gradient_sum)


def tdot(a, b):
    return lax.dot_general(a, b, (((0,), (0,)), ((), ())), preferred_element_type=jnp.float32)


def dott(a, b):
    return lax.dot_general(a, b, (((1,), (1,)), ((), ())), preferred_element_type=jnp.float32)


def after(array, *others):
    return lax.optimization_barrier((array,) + others)[0]


def two_side_shards(sizes):
    groups, layers, sides, cores = sizes
    places = [(g, z, s, c) for g in range(groups) for z in range(layers) for s in range(sides) for c in range(cores)]
    index = {place: i for i, place in enumerate(places)}

    def pairs(move, chosen=lambda g, z, s, c: True):
        return [(index[p], index[move(*p)]) for p in places if chosen(*p)]

    def is_home(g, z, s, c):
        return z // 2 == s

    def jumped(g, z, s, c):
        return (g, z ^ 2, s, c)

    cross_pairs = pairs(lambda g, z, s, c: (g, z, 1 - s, c))
    step_pairs = pairs(lambda g, z, s, c: (g, z ^ 1, s, c))
    core_pairs = pairs(lambda g, z, s, c: (g, z, s, 1 - c))
    jump_pairs, home_jump_pairs = pairs(jumped), pairs(jumped, is_home)

    def cross(a):
        return lax.ppermute(a, AXES, cross_pairs)

    def step(a):
        return lax.ppermute(a, AXES, step_pairs)

    def swap(a):
        return lax.ppermute(a, AXES, core_pairs)

    def home_jump(a):
        return lax.ppermute(a, AXES, home_jump_pairs)

    def jump(a):
        return lax.ppermute(a, AXES, jump_pairs)

    def shards(expected_cot, value_next, transition, section):
        df = factor_of(section)
        z, s, c = lax.axis_index("markov"), lax.axis_index("storage"), lax.axis_index("sub")
        home = z // 2 == s
        mine = z % 2 == c
        half = expected_cot.shape[1] // 2
        quarter = half // 2

        def columns(array, start, stop):
            return array[:, start * quarter : stop * quarter]

        def together(arrays, *gates):
            return lax.optimization_barrier(tuple(arrays) + gates)[: len(arrays)]

        e = [columns(expected_cot, i, i + 1) for i in range(4)]
        v = [columns(value_next, i, i + 1) for i in range(4)]
        x1 = cross(jnp.where(home, v[0], e[0]))
        t_other = swap(transition)
        e2 = after(e[2], x1)
        j1 = jump(jnp.where(home, x1, e2))
        t_near, t_next = jnp.where(mine, transition, t_other), jnp.where(mine, t_other, transition)

        def adjoint_of(near, far):
            return tdot(t_near, near) + tdot(t_next, far)

        v1, e1 = together((v[1], e[1]), x1, t_near)
        x2 = cross(jnp.concatenate([jnp.where(home, v1, e1), v[2]], 1))
        x2, v_across2 = columns(x2, 0, 1), columns(x2, 1, 2)
        second = jnp.where(home, x2, e[3])
        j2 = jump(second)
        near, far = together((j1, v[0]), second)
        third_cross = jnp.where(home, near, far)
        x3 = cross(jnp.concatenate([third_cross, v[3]], 1))
        x3, v_across3 = columns(x3, 0, 1), columns(x3, 1, 2)
        near, far = together((x1, j1), third_cross)
        b0 = jnp.where(home, near, far)
        b0_next = step(b0)
        third = jnp.where(home, e[0], x3)
        j3 = jump(third)
        sum0 = adjoint_of(b0, b0_next)
        near, far = together((j2, v[1]), third)
        x4 = cross(jnp.where(home, near, far))
        near, far = together((x2, j2), sum0, third)
        b1 = jnp.where(home, near, far)
        b1_next = step(b1)
        part0 = cross(after(sum0, x4))
        near, far = together((e[1], x4), j3)
        fourth = jnp.where(home, near, far)
        j4 = jump(fourth)
        sum1 = adjoint_of(b1, b1_next)
        part1 = cross(after(sum1, part0))
        near, both, far = together((e[0], j3, x3), sum1, x4)
        a0b2 = jnp.where(home, jnp.concatenate([near, both], 1), jnp.concatenate([both, far], 1))
        a0b2_next = step(a0b2)
        sum2 = adjoint_of(columns(a0b2, 1, 2), columns(after(a0b2_next, part1), 1, 2))
        part2 = cross(sum2)
        j5 = home_jump(after(columns(expected_cot, 2, 4), j3))
        near, both, far = together((e[1], j4, x4), a0b2_next, part0)
        a1b3 = jnp.where(home, jnp.concatenate([near, both], 1), jnp.concatenate([both, far], 1))
        a1b3_next = step(a1b3)
        v_other = swap(after(value_next, sum1))
        sum3 = adjoint_of(columns(a1b3, 1, 2), columns(after(a1b3_next, part2), 1, 2))
        part3 = cross(sum3)

        def product(near, far, values, values_other):
            own, swapped = jnp.where(mine, near, far), swap(jnp.where(mine, far, near))
            return dott(jnp.concatenate([own, swapped], 1), jnp.concatenate(values + values_other, 1))

        parts = together((x1, x2, x3, x4, v_across2, v_across3), sum1)
        v_across = jnp.concatenate(
            [jnp.where(home, parts[2], parts[0]), jnp.where(home, parts[3], parts[1]), parts[4], parts[5]], 1
        )
        v_across_other = swap(v_across)
        w, w_other, u, u_other = (
            [columns(array, i, i + 1) for i in range(4)] for array in (value_next, v_other, v_across, v_across_other)
        )
        early = together((b0, b1, a0b2, b0_next, b1_next, a0b2_next), a1b3, sum2)
        grad = product(
            jnp.concatenate(early[:3], 1),
            jnp.concatenate(early[3:], 1),
            [u[0], u[1], w[0], u[2]],
            [u_other[0], u_other[1], w_other[0], u_other[2]],
        )
        near, far = together((columns(expected_cot, 2, 4), j5), a1b3_next, part1, grad)
        a23 = jnp.where(home, near, far)
        a23_next = step(a23)
        near, far = together((a1b3, a1b3_next), a23, sum3)
        grad = grad + product(near, far, [w[1], u[3]], [w_other[1], u_other[3]])
        own01 = adjoint_of(
            jnp.concatenate([columns(a0b2, 0, 1), columns(near, 0, 1)], 1),
            jnp.concatenate([columns(a0b2_next, 0, 1), columns(far, 0, 1)], 1),
        )
        near, far = together((a23, a23_next), grad, own01)
        grad = df * (grad + product(near, far, [w[2], w[3]], [w_other[2], w_other[3]]))
        own23 = adjoint_of(near, far)
        own23, part3, grad = together((own23, part3, grad))
        adjoint = df * (
            jnp.concatenate([own01, own23], 1) + jnp.concatenate([part0, part1, part2, part3], 1)
        )
        return adjoint, grad

    return shards


def solution(mesh):
    sizes = tuple(mesh.shape[a] for a in AXES)
    shards = two_side_shards(sizes) if sizes[1:] == (4, 2, 2) else plain_shards
    return jax.shard_map(
        shards,
        mesh=mesh,
        in_specs=(
            P(("groups", "markov"), ("storage", "sub")),
            P(("groups", "markov"), ("storage", "sub")),
            P(("groups", "storage", "sub"), "markov"),
            P("groups"),
        ),
        out_specs=(
            P(("groups", "markov"), ("storage", "sub")),
            P(("groups", "storage", "sub"), "markov"),
        ),
        check_vma=False,
    )
```

```python
import jax
import jax.numpy as jnp
from jax import lax
from jax.sharding import PartitionSpec as P

discount_rate = 0.97
AXES = ("groups", "markov", "storage", "sub")


def factor_of(section):
    return jnp.exp(section[0].astype(jnp.float32) * jnp.log(jnp.float32(discount_rate)))


def plain_shards(expected_cot, value_next, transition, section):
    discount_factor = factor_of(section)
    cotangent_all = lax.all_gather(expected_cot, "markov", axis=0, tiled=True)
    adjoint_sum = lax.dot_general(
        lax.all_gather(transition, ("storage", "sub"), axis=0, tiled=True),
        cotangent_all,
        (((0,), (0,)), ((), ())),
        preferred_element_type=jnp.float32,
    )
    own_states = lax.all_to_all(
        cotangent_all, ("storage", "sub"), split_axis=0, concat_axis=1, tiled=True
    )
    gathered_values = lax.all_gather(value_next, ("storage", "sub"), axis=1, tiled=True)
    gradient_sum = lax.dot_general(
        own_states, gathered_values, (((1,), (1,)), ((), ())), preferred_element_type=jnp.float32
    )
    return (discount_factor * adjoint_sum, discount_factor * gradient_sum)


def tdot(a, b):
    return lax.dot_general(a, b, (((0,), (0,)), ((), ())), preferred_element_type=jnp.float32)


def dott(a, b):
    return lax.dot_general(a, b, (((1,), (1,)), ((), ())), preferred_element_type=jnp.float32)


def after(array, *others):
    return lax.optimization_barrier((array,) + others)[0]


def two_side_shards(sizes):
    groups, layers, sides, cores = sizes
    places = [(g, z, s, c) for g in range(groups) for z in range(layers) for s in range(sides) for c in range(cores)]
    index = {place: i for i, place in enumerate(places)}

    def pairs(move, chosen=lambda g, z, s, c: True):
        return [(index[p], index[move(*p)]) for p in places if chosen(*p)]

    def is_home(g, z, s, c):
        return z // 2 == s

    def jumped(g, z, s, c):
        return (g, z ^ 2, s, c)

    cross_pairs = pairs(lambda g, z, s, c: (g, z, 1 - s, c))
    step_pairs = pairs(lambda g, z, s, c: (g, z ^ 1, s, c))
    core_pairs = pairs(lambda g, z, s, c: (g, z, s, 1 - c))
    jump_pairs, home_jump_pairs = pairs(jumped), pairs(jumped, is_home)

    def cross(a):
        return lax.ppermute(a, AXES, cross_pairs)

    def step(a):
        return lax.ppermute(a, AXES, step_pairs)

    def swap(a):
        return lax.ppermute(a, AXES, core_pairs)

    def home_jump(a):
        return lax.ppermute(a, AXES, home_jump_pairs)

    def jump(a):
        return lax.ppermute(a, AXES, jump_pairs)

    def shards(expected_cot, value_next, transition, section):
        df = factor_of(section)
        z, s, c = lax.axis_index("markov"), lax.axis_index("storage"), lax.axis_index("sub")
        home = z // 2 == s
        mine = z % 2 == c
        half = expected_cot.shape[1] // 2
        quarter = half // 2

        def columns(array, start, stop):
            return array[:, start * quarter : stop * quarter]

        def together(arrays, *gates):
            return lax.optimization_barrier(tuple(arrays) + gates)[: len(arrays)]

        e = [columns(expected_cot, i, i + 1) for i in range(4)]
        v = [columns(value_next, i, i + 1) for i in range(4)]
        x1 = cross(jnp.where(home, v[0], e[0]))
        t_other = swap(transition)
        e2 = after(e[2], x1)
        j1 = jump(jnp.where(home, x1, e2))
        t_near, t_next = jnp.where(mine, transition, t_other), jnp.where(mine, t_other, transition)

        def adjoint_of(near, far):
            return tdot(t_near, near) + tdot(t_next, far)

        v1, e1 = together((v[1], e[1]), x1, t_near)
        x2 = cross(jnp.concatenate([jnp.where(home, v1, e1), v[2]], 1))
        x2, v_across2 = columns(x2, 0, 1), columns(x2, 1, 2)
        second = jnp.where(home, x2, e[3])
        j2 = jump(second)
        near, far = together((j1, v[0]), second)
        third_cross = jnp.where(home, near, far)
        x3 = cross(jnp.concatenate([third_cross, v[3]], 1))
        x3, v_across3 = columns(x3, 0, 1), columns(x3, 1, 2)
        near, far = together((x1, j1), third_cross)
        b0 = jnp.where(home, near, far)
        b0_next = step(b0)
        third = jnp.where(home, e[0], x3)
        j3 = jump(third)
        sum0 = adjoint_of(b0, b0_next)
        near, far = together((j2, v[1]), third)
        x4 = cross(jnp.where(home, near, far))
        near, far = together((x2, j2), sum0, third)
        b1 = jnp.where(home, near, far)
        b1_next = step(b1)
        part0 = cross(after(sum0, x4))
        fourth = jnp.where(home, e[1], x4)
        j4 = jump(fourth)
        sum1 = adjoint_of(b1, b1_next)
        part1 = cross(after(sum1, part0))
        near, both, far = together((e[0], j3, x3), sum1, fourth)
        a0b2 = jnp.where(home, jnp.concatenate([near, both], 1), jnp.concatenate([both, far], 1))
        a0b2_next = step(a0b2)
        sum2 = adjoint_of(columns(a0b2, 1, 2), columns(a0b2_next, 1, 2))
        part2 = cross(after(sum2, part1))
        j5 = home_jump(after(columns(expected_cot, 2, 4), j3))
        near, both, far = together((e[1], j4, x4), sum2, part0)
        a1b3 = jnp.where(home, jnp.concatenate([near, both], 1), jnp.concatenate([both, far], 1))
        a1b3_next = step(a1b3)
        v_other = swap(after(value_next, sum1))
        sum3 = adjoint_of(columns(a1b3, 1, 2), columns(a1b3_next, 1, 2))
        part3 = cross(after(sum3, part2))

        def own_and_swapped(near, far):
            return jnp.where(mine, near, far), swap(jnp.where(mine, far, near))

        parts = together((x1, x2, x3, x4, v_across2, v_across3), sum1)
        v_across = jnp.concatenate(
            [jnp.where(home, parts[2], parts[0]), jnp.where(home, parts[3], parts[1]), parts[4], parts[5]], 1
        )
        v_across_other = swap(v_across)
        near, far = together((columns(expected_cot, 2, 4), j5), a1b3_next, part1)
        a23 = jnp.where(home, near, far)
        a23_next = step(a23)
        b0, b0_next, b1, b1_next, a0b2, a0b2_next = together(
            (b0, b0_next, b1, b1_next, a0b2, a0b2_next), a1b3_next, sum3, part2, a23
        )
        a0, a0_next = columns(a0b2, 0, 1), columns(a0b2_next, 0, 1)
        a1, a1_next = columns(a1b3, 0, 1), columns(a1b3_next, 0, 1)
        b_own, b_swapped = own_and_swapped(
            jnp.concatenate([b0, b1, columns(a0b2, 1, 2), columns(a1b3, 1, 2)], 1),
            jnp.concatenate([b0_next, b1_next, columns(a0b2_next, 1, 2), columns(a1b3_next, 1, 2)], 1),
        )
        a01_own, a01_swapped = own_and_swapped(
            jnp.concatenate([a0, a1], 1), jnp.concatenate([a0_next, a1_next], 1)
        )
        grad = dott(
            jnp.concatenate([b_own, b_swapped], 1), jnp.concatenate([v_across, v_across_other], 1)
        ) + dott(
            jnp.concatenate([a01_own, a01_swapped], 1),
            jnp.concatenate([columns(value_next, 0, 2), columns(v_other, 0, 2)], 1),
        )
        own01 = adjoint_of(jnp.concatenate([a0, a1], 1), jnp.concatenate([a0_next, a1_next], 1))
        near, far = together((a23, a23_next), grad, own01)
        a23_own, a23_swapped = own_and_swapped(near, far)
        grad = df * (grad + dott(
            jnp.concatenate([a23_own, a23_swapped], 1),
            jnp.concatenate([columns(value_next, 2, 4), columns(v_other, 2, 4)], 1),
        ))
        own23 = adjoint_of(near, far)
        own23, part3, grad = together((own23, part3, grad))
        adjoint = df * (
            jnp.concatenate([own01, own23], 1) + jnp.concatenate([part0, part1, part2, part3], 1)
        )
        return adjoint, grad

    return shards


def solution(mesh):
    sizes = tuple(mesh.shape[a] for a in AXES)
    shards = two_side_shards(sizes) if sizes[1:] == (4, 2, 2) else plain_shards
    return jax.shard_map(
        shards,
        mesh=mesh,
        in_specs=(
            P(("groups", "markov"), ("storage", "sub")),
            P(("groups", "markov"), ("storage", "sub")),
            P(("groups", "storage", "sub"), "markov"),
            P("groups"),
        ),
        out_specs=(
            P(("groups", "markov"), ("storage", "sub")),
            P(("groups", "storage", "sub"), "markov"),
        ),
        check_vma=False,
    )
```

```python
import jax
import jax.numpy as jnp
from jax import lax
from jax.sharding import PartitionSpec as P

discount_rate = 0.97
AXES = ("groups", "markov", "storage", "sub")


def factor_of(section):
    return jnp.exp(section[0].astype(jnp.float32) * jnp.log(jnp.float32(discount_rate)))


def plain_shards(expected_cot, value_next, transition, section):
    discount_factor = factor_of(section)
    cotangent_all = lax.all_gather(expected_cot, "markov", axis=0, tiled=True)
    adjoint_sum = lax.dot_general(
        lax.all_gather(transition, ("storage", "sub"), axis=0, tiled=True),
        cotangent_all,
        (((0,), (0,)), ((), ())),
        preferred_element_type=jnp.float32,
    )
    own_states = lax.all_to_all(
        cotangent_all, ("storage", "sub"), split_axis=0, concat_axis=1, tiled=True
    )
    gathered_values = lax.all_gather(value_next, ("storage", "sub"), axis=1, tiled=True)
    gradient_sum = lax.dot_general(
        own_states, gathered_values, (((1,), (1,)), ((), ())), preferred_element_type=jnp.float32
    )
    return (discount_factor * adjoint_sum, discount_factor * gradient_sum)


def tdot(a, b):
    return lax.dot_general(a, b, (((0,), (0,)), ((), ())), preferred_element_type=jnp.float32)


def dott(a, b):
    return lax.dot_general(a, b, (((1,), (1,)), ((), ())), preferred_element_type=jnp.float32)


def after(array, *others):
    return lax.optimization_barrier((array,) + others)[0]


def two_side_shards(sizes):
    groups, layers, sides, cores = sizes
    places = [(g, z, s, c) for g in range(groups) for z in range(layers) for s in range(sides) for c in range(cores)]
    index = {place: i for i, place in enumerate(places)}

    def pairs(move, chosen=lambda g, z, s, c: True):
        return [(index[p], index[move(*p)]) for p in places if chosen(*p)]

    def is_home(g, z, s, c):
        return z // 2 == s

    def jumped(g, z, s, c):
        return (g, z ^ 2, s, c)

    cross_pairs = pairs(lambda g, z, s, c: (g, z, 1 - s, c))
    step_pairs = pairs(lambda g, z, s, c: (g, z ^ 1, s, c))
    core_pairs = pairs(lambda g, z, s, c: (g, z, s, 1 - c))
    jump_pairs, home_jump_pairs = pairs(jumped), pairs(jumped, is_home)

    def cross(a):
        return lax.ppermute(a, AXES, cross_pairs)

    def step(a):
        return lax.ppermute(a, AXES, step_pairs)

    def swap(a):
        return lax.ppermute(a, AXES, core_pairs)

    def home_jump(a):
        return lax.ppermute(a, AXES, home_jump_pairs)

    def jump(a):
        return lax.ppermute(a, AXES, jump_pairs)

    def shards(expected_cot, value_next, transition, section):
        df = factor_of(section)
        z, s, c = lax.axis_index("markov"), lax.axis_index("storage"), lax.axis_index("sub")
        home = z // 2 == s
        mine = z % 2 == c
        half = expected_cot.shape[1] // 2
        quarter = half // 2

        def columns(array, start, stop):
            return array[:, start * quarter : stop * quarter]

        def together(arrays, *gates):
            return lax.optimization_barrier(tuple(arrays) + gates)[: len(arrays)]

        e = [columns(expected_cot, i, i + 1) for i in range(4)]
        v = [columns(value_next, i, i + 1) for i in range(4)]
        x1 = cross(jnp.where(home, v[0], e[0]))
        t_other = swap(transition)
        e2 = after(e[2], x1)
        j1 = jump(jnp.where(home, x1, e2))
        t_near, t_next = jnp.where(mine, transition, t_other), jnp.where(mine, t_other, transition)

        def adjoint_of(near, far):
            return tdot(t_near, near) + tdot(t_next, far)

        v1, e1 = together((v[1], e[1]), x1, t_near)
        x2 = cross(jnp.concatenate([jnp.where(home, v1, e1), v[2]], 1))
        x2, v_across2 = columns(x2, 0, 1), columns(x2, 1, 2)
        second = jnp.where(home, x2, e[3])
        j2 = jump(second)
        near, far = together((j1, v[0]), second)
        third_cross = jnp.where(home, near, far)
        x3 = cross(jnp.concatenate([third_cross, v[3]], 1))
        x3, v_across3 = columns(x3, 0, 1), columns(x3, 1, 2)
        near, far = together((x1, j1), third_cross)
        b0 = jnp.where(home, near, far)
        b0_next = step(b0)
        third = jnp.where(home, e[0], x3)
        j3 = jump(third)
        sum0 = adjoint_of(b0, b0_next)
        near, far = together((j2, v[1]), third)
        x4 = cross(jnp.where(home, near, far))
        near, far = together((x2, j2), sum0, third)
        b1 = jnp.where(home, near, far)
        b1_next = step(b1)
        part0 = cross(after(sum0, x4))
        near, far = together((e[1], x4), j3)
        fourth = jnp.where(home, near, far)
        j4 = jump(fourth)
        sum1 = adjoint_of(b1, b1_next)
        part1 = cross(after(sum1, part0))
        near, far = together((j3, x3), sum1, x4)
        b2 = jnp.where(home, near, far)
        b2_next = step(b2)
        sum2 = adjoint_of(b2, b2_next)
        part2 = cross(after(sum2, part1))
        j5 = home_jump(after(columns(expected_cot, 2, 4), j3))
        near, far = together((e[0], j3), b2_next, part0)
        a0 = jnp.where(home, near, far)
        a0_next = step(a0)
        near, far = together((j4, x4), sum2, part0, a0_next)
        b3 = jnp.where(home, near, far)
        b3_next = step(b3)
        v_other = swap(after(value_next, sum1))
        sum3 = adjoint_of(b3, b3_next)
        part3 = cross(after(sum3, part2))
        near, far = together((e[1], j4), sum3)
        a1 = jnp.where(home, near, far)
        a1_next = step(a1)

        def own_and_swapped(near, far):
            return jnp.where(mine, near, far), swap(jnp.where(mine, far, near))

        parts = together((x1, x2, x3, x4, v_across2, v_across3), sum1)
        v_across = jnp.concatenate(
            [jnp.where(home, parts[2], parts[0]), jnp.where(home, parts[3], parts[1]), parts[4], parts[5]], 1
        )
        v_across_other = swap(v_across)
        near, far = together((columns(expected_cot, 2, 4), j5), a1_next, sum3, part2)
        a23 = jnp.where(home, near, far)
        a23_next = step(a23)
        near = together((b0, b1, b2, b3), sum3, part2)
        far = together((b0_next, b1_next, b2_next, b3_next), sum3, part2)
        b_own, b_swapped = own_and_swapped(jnp.concatenate(near, 1), jnp.concatenate(far, 1))
        a0, a0_next, a1, a1_next = together((a0, a0_next, a1, a1_next), a23)
        a01_own, a01_swapped = own_and_swapped(
            jnp.concatenate([a0, a1], 1), jnp.concatenate([a0_next, a1_next], 1)
        )
        grad = dott(
            jnp.concatenate([b_own, b_swapped], 1), jnp.concatenate([v_across, v_across_other], 1)
        ) + dott(
            jnp.concatenate([a01_own, a01_swapped], 1),
            jnp.concatenate([columns(value_next, 0, 2), columns(v_other, 0, 2)], 1),
        )
        own01 = adjoint_of(jnp.concatenate([a0, a1], 1), jnp.concatenate([a0_next, a1_next], 1))
        near, far = together((a23, a23_next), grad, own01)
        a23_own, a23_swapped = own_and_swapped(near, far)
        grad = df * (grad + dott(
            jnp.concatenate([a23_own, a23_swapped], 1),
            jnp.concatenate([columns(value_next, 2, 4), columns(v_other, 2, 4)], 1),
        ))
        own23 = adjoint_of(near, far)
        adjoint = df * (
            jnp.concatenate([own01, own23], 1) + jnp.concatenate([part0, part1, part2, part3], 1)
        )
        return adjoint, grad

    return shards


def solution(mesh):
    sizes = tuple(mesh.shape[a] for a in AXES)
    shards = two_side_shards(sizes) if sizes[1:] == (4, 2, 2) else plain_shards
    return jax.shard_map(
        shards,
        mesh=mesh,
        in_specs=(
            P(("groups", "markov"), ("storage", "sub")),
            P(("groups", "markov"), ("storage", "sub")),
            P(("groups", "storage", "sub"), "markov"),
            P("groups"),
        ),
        out_specs=(
            P(("groups", "markov"), ("storage", "sub")),
            P(("groups", "storage", "sub"), "markov"),
        ),
        check_vma=False,
    )
```

```python
import jax
import jax.numpy as jnp
from jax import lax
from jax.sharding import PartitionSpec as P

discount_rate = 0.97
AXES = ("groups", "markov", "storage", "sub")


def factor_of(section):
    return jnp.exp(section[0].astype(jnp.float32) * jnp.log(jnp.float32(discount_rate)))


def plain_shards(expected_cot, value_next, transition, section):
    discount_factor = factor_of(section)
    cotangent_all = lax.all_gather(expected_cot, "markov", axis=0, tiled=True)
    adjoint_sum = lax.dot_general(
        lax.all_gather(transition, ("storage", "sub"), axis=0, tiled=True),
        cotangent_all,
        (((0,), (0,)), ((), ())),
        preferred_element_type=jnp.float32,
    )
    own_states = lax.all_to_all(
        cotangent_all, ("storage", "sub"), split_axis=0, concat_axis=1, tiled=True
    )
    gathered_values = lax.all_gather(value_next, ("storage", "sub"), axis=1, tiled=True)
    gradient_sum = lax.dot_general(
        own_states, gathered_values, (((1,), (1,)), ((), ())), preferred_element_type=jnp.float32
    )
    return (discount_factor * adjoint_sum, discount_factor * gradient_sum)


def tdot(a, b):
    return lax.dot_general(a, b, (((0,), (0,)), ((), ())), preferred_element_type=jnp.float32)


def dott(a, b):
    return lax.dot_general(a, b, (((1,), (1,)), ((), ())), preferred_element_type=jnp.float32)


def after(array, *others):
    return lax.optimization_barrier((array,) + others)[0]


def two_side_shards(sizes):
    groups, layers, sides, cores = sizes
    places = [(g, z, s, c) for g in range(groups) for z in range(layers) for s in range(sides) for c in range(cores)]
    index = {place: i for i, place in enumerate(places)}

    def pairs(move, chosen=lambda g, z, s, c: True):
        return [(index[p], index[move(*p)]) for p in places if chosen(*p)]

    def is_home(g, z, s, c):
        return z // 2 == s

    def jumped(g, z, s, c):
        return (g, z ^ 2, s, c)

    cross_pairs = pairs(lambda g, z, s, c: (g, z, 1 - s, c))
    step_pairs = pairs(lambda g, z, s, c: (g, z ^ 1, s, c))
    core_pairs = pairs(lambda g, z, s, c: (g, z, s, 1 - c))
    jump_pairs, home_jump_pairs = pairs(jumped), pairs(jumped, is_home)

    def cross(a):
        return lax.ppermute(a, AXES, cross_pairs)

    def step(a):
        return lax.ppermute(a, AXES, step_pairs)

    def swap(a):
        return lax.ppermute(a, AXES, core_pairs)

    def home_jump(a):
        return lax.ppermute(a, AXES, home_jump_pairs)

    def jump(a):
        return lax.ppermute(a, AXES, jump_pairs)

    def shards(expected_cot, value_next, transition, section):
        df = factor_of(section)
        z, s, c = lax.axis_index("markov"), lax.axis_index("storage"), lax.axis_index("sub")
        home = z // 2 == s
        mine = z % 2 == c
        half = expected_cot.shape[1] // 2
        quarter = half // 2

        def columns(array, start, stop):
            return array[:, start * quarter : stop * quarter]

        def together(arrays, *gates):
            return lax.optimization_barrier(tuple(arrays) + gates)[: len(arrays)]

        first = jnp.where(home, columns(value_next, 0, 1), columns(expected_cot, 0, 1))
        x1 = cross(first)
        expected_cot, value_next, transition = together((expected_cot, value_next, transition), first)
        e = [columns(expected_cot, i, i + 1) for i in range(4)]
        v = [columns(value_next, i, i + 1) for i in range(4)]
        t_other = swap(transition)
        t_near, t_next = jnp.where(mine, transition, t_other), jnp.where(mine, t_other, transition)
        first_jump = jnp.where(home, x1, after(e[2], x1, t_near))
        j1 = jump(first_jump)

        def adjoint_of(near, far):
            return tdot(t_near, near) + tdot(t_next, far)

        v1, e1 = together((v[1], e[1]), x1, t_near)
        x2 = cross(jnp.concatenate([jnp.where(home, v1, e1), v[2]], 1))
        x2, v_across2 = columns(x2, 0, 1), columns(x2, 1, 2)
        second = jnp.where(home, x2, columns(after(expected_cot, first_jump), 3, 4))
        j2 = jump(second)
        near, far = together((j1, v[0]), second)
        third_cross = jnp.where(home, near, far)
        x3 = cross(jnp.concatenate([third_cross, v[3]], 1))
        x3, v_across3 = columns(x3, 0, 1), columns(x3, 1, 2)
        near, far = together((x1, j1), third_cross)
        b0 = jnp.where(home, near, far)
        b0_next = step(b0)
        third = jnp.where(home, e[0], x3)
        j3 = jump(third)
        sum0 = adjoint_of(b0, b0_next)
        near, far = together((j2, v[1]), third)
        x4 = cross(jnp.where(home, near, far))
        near, far = together((x2, j2), sum0, third)
        b1 = jnp.where(home, near, far)
        b1_next = step(b1)
        part0 = cross(after(sum0, x4))
        fourth = jnp.where(home, e[1], x4)
        j4 = jump(fourth)
        sum1 = adjoint_of(b1, b1_next)
        part1 = cross(after(sum1, part0))
        near, both, far = together((e[0], j3, x3), sum1, fourth)
        a0b2 = jnp.where(home, jnp.concatenate([near, both], 1), jnp.concatenate([both, far], 1))
        a0b2_next = step(a0b2)
        sum2 = adjoint_of(columns(a0b2, 1, 2), columns(a0b2_next, 1, 2))
        part2 = cross(after(sum2, part1))
        j5 = home_jump(after(columns(expected_cot, 2, 4), j3))
        near, both, far = together((e[1], j4, x4), sum2, part0)
        a1b3 = jnp.where(home, jnp.concatenate([near, both], 1), jnp.concatenate([both, far], 1))
        a1b3_next = step(a1b3)
        v_other = swap(after(value_next, sum1))
        sum3 = adjoint_of(columns(a1b3, 1, 2), columns(a1b3_next, 1, 2))
        part3 = cross(after(sum3, part2))

        def own_and_swapped(near, far):
            return jnp.where(mine, near, far), swap(jnp.where(mine, far, near))

        parts = together((x1, x2, x3, x4, v_across2, v_across3), sum1)
        v_across = jnp.concatenate(
            [jnp.where(home, parts[2], parts[0]), jnp.where(home, parts[3], parts[1]), parts[4], parts[5]], 1
        )
        v_across_other = swap(v_across)
        near, far = together((columns(expected_cot, 2, 4), j5), a1b3_next, part1)
        a23 = jnp.where(home, near, far)
        a23_next = step(a23)
        b0, b0_next, b1, b1_next, a0b2, a0b2_next = together(
            (b0, b0_next, b1, b1_next, a0b2, a0b2_next), a1b3_next, sum3, part2, a23
        )
        a0, a0_next = columns(a0b2, 0, 1), columns(a0b2_next, 0, 1)
        a1, a1_next = columns(a1b3, 0, 1), columns(a1b3_next, 0, 1)
        b_own, b_swapped = own_and_swapped(
            jnp.concatenate([b0, b1, columns(a0b2, 1, 2), columns(a1b3, 1, 2)], 1),
            jnp.concatenate([b0_next, b1_next, columns(a0b2_next, 1, 2), columns(a1b3_next, 1, 2)], 1),
        )
        a01_own, a01_swapped = own_and_swapped(
            jnp.concatenate([a0, a1], 1), jnp.concatenate([a0_next, a1_next], 1)
        )
        grad = dott(
            jnp.concatenate([b_own, b_swapped], 1), jnp.concatenate([v_across, v_across_other], 1)
        ) + dott(
            jnp.concatenate([a01_own, a01_swapped], 1),
            jnp.concatenate([columns(value_next, 0, 2), columns(v_other, 0, 2)], 1),
        )
        own01 = adjoint_of(jnp.concatenate([a0, a1], 1), jnp.concatenate([a0_next, a1_next], 1))
        near, far = together((a23, a23_next), grad, own01)
        a23_own, a23_swapped = own_and_swapped(near, far)
        grad = df * (grad + dott(
            jnp.concatenate([a23_own, a23_swapped], 1),
            jnp.concatenate([columns(value_next, 2, 4), columns(v_other, 2, 4)], 1),
        ))
        own23 = adjoint_of(near, far)
        own23, part3, grad = together((own23, part3, grad))
        adjoint = df * (
            jnp.concatenate([own01, own23], 1) + jnp.concatenate([part0, part1, part2, part3], 1)
        )
        return adjoint, grad

    return shards


def solution(mesh):
    sizes = tuple(mesh.shape[a] for a in AXES)
    shards = two_side_shards(sizes) if sizes[1:] == (4, 2, 2) else plain_shards
    return jax.shard_map(
        shards,
        mesh=mesh,
        in_specs=(
            P(("groups", "markov"), ("storage", "sub")),
            P(("groups", "markov"), ("storage", "sub")),
            P(("groups", "storage", "sub"), "markov"),
            P("groups"),
        ),
        out_specs=(
            P(("groups", "markov"), ("storage", "sub")),
            P(("groups", "storage", "sub"), "markov"),
        ),
        check_vma=False,
    )
```

```python
import jax
import jax.numpy as jnp
from jax import lax
from jax.sharding import PartitionSpec as P

discount_rate = 0.97
AXES = ("groups", "markov", "storage", "sub")


def factor_of(section):
    return jnp.exp(section[0].astype(jnp.float32) * jnp.log(jnp.float32(discount_rate)))


def plain_shards(expected_cot, value_next, transition, section):
    discount_factor = factor_of(section)
    cotangent_all = lax.all_gather(expected_cot, "markov", axis=0, tiled=True)
    adjoint_sum = lax.dot_general(
        lax.all_gather(transition, ("storage", "sub"), axis=0, tiled=True),
        cotangent_all,
        (((0,), (0,)), ((), ())),
        preferred_element_type=jnp.float32,
    )
    own_states = lax.all_to_all(
        cotangent_all, ("storage", "sub"), split_axis=0, concat_axis=1, tiled=True
    )
    gathered_values = lax.all_gather(value_next, ("storage", "sub"), axis=1, tiled=True)
    gradient_sum = lax.dot_general(
        own_states, gathered_values, (((1,), (1,)), ((), ())), preferred_element_type=jnp.float32
    )
    return (discount_factor * adjoint_sum, discount_factor * gradient_sum)


def tdot(a, b):
    return lax.dot_general(a, b, (((0,), (0,)), ((), ())), preferred_element_type=jnp.float32)


def dott(a, b):
    return lax.dot_general(a, b, (((1,), (1,)), ((), ())), preferred_element_type=jnp.float32)


def after(array, *others):
    return lax.optimization_barrier((array,) + others)[0]


def two_side_shards(sizes):
    groups, layers, sides, cores = sizes
    places = [(g, z, s, c) for g in range(groups) for z in range(layers) for s in range(sides) for c in range(cores)]
    index = {place: i for i, place in enumerate(places)}

    def pairs(move, chosen=lambda g, z, s, c: True):
        return [(index[p], index[move(*p)]) for p in places if chosen(*p)]

    def is_home(g, z, s, c):
        return z // 2 == s

    def jumped(g, z, s, c):
        return (g, z ^ 2, s, c)

    cross_pairs = pairs(lambda g, z, s, c: (g, z, 1 - s, c))
    step_pairs = pairs(lambda g, z, s, c: (g, z ^ 1, s, c))
    core_pairs = pairs(lambda g, z, s, c: (g, z, s, 1 - c))
    jump_pairs, home_jump_pairs = pairs(jumped), pairs(jumped, is_home)

    def cross(a):
        return lax.ppermute(a, AXES, cross_pairs)

    def step(a):
        return lax.ppermute(a, AXES, step_pairs)

    def swap(a):
        return lax.ppermute(a, AXES, core_pairs)

    def home_jump(a):
        return lax.ppermute(a, AXES, home_jump_pairs)

    def jump(a):
        return lax.ppermute(a, AXES, jump_pairs)

    def shards(expected_cot, value_next, transition, section):
        df = factor_of(section)
        z, s, c = lax.axis_index("markov"), lax.axis_index("storage"), lax.axis_index("sub")
        home = z // 2 == s
        mine = z % 2 == c
        half = expected_cot.shape[1] // 2
        quarter = half // 2

        def columns(array, start, stop):
            return array[:, start * quarter : stop * quarter]

        def together(arrays, *gates):
            return lax.optimization_barrier(tuple(arrays) + gates)[: len(arrays)]

        e = [columns(expected_cot, i, i + 1) for i in range(4)]
        v = [columns(value_next, i, i + 1) for i in range(4)]
        x1 = cross(jnp.where(home, v[0], e[0]))
        rows = e[3].shape[0] // 2
        j0 = home_jump(e[3][:rows])
        t_other = swap(transition)
        e2 = after(e[2], x1)
        j1 = jump(jnp.where(home, x1, e2))
        t_near, t_next = jnp.where(mine, transition, t_other), jnp.where(mine, t_other, transition)

        def adjoint_of(near, far):
            return tdot(t_near, near) + tdot(t_next, far)

        v1, e1 = together((v[1], e[1]), x1, t_near, j0)
        x2 = cross(jnp.concatenate([jnp.where(home, v1, e1), v[2]], 1))
        x2, v_across2 = columns(x2, 0, 1), columns(x2, 1, 2)
        near, far = together((e[3][:rows], j0), x1)
        a3_top = jnp.where(home, near, far)
        a3_top_next = step(a3_top)
        second = jnp.where(home, x2, e[3])
        j2 = jump(second)
        near, far = together((j1, v[0]), second)
        third_cross = jnp.where(home, near, far)
        x3 = cross(jnp.concatenate([third_cross, v[3]], 1))
        x3, v_across3 = columns(x3, 0, 1), columns(x3, 1, 2)
        near, far = together((x1, j1), third_cross, a3_top_next)
        b0 = jnp.where(home, near, far)
        b0_next = step(b0)
        third = jnp.where(home, e[0], x3)
        j3 = jump(third)
        sum0 = adjoint_of(b0, b0_next)
        near, far = together((j2, v[1]), third)
        x4 = cross(jnp.where(home, near, far))
        near, far = together((x2, j2), sum0, third)
        b1 = jnp.where(home, near, far)
        b1_next = step(b1)
        part0 = cross(after(sum0, x4))
        fourth = jnp.where(home, e[1], x4)
        j4 = jump(fourth)
        sum1 = adjoint_of(b1, b1_next)
        part1 = cross(after(sum1, part0))
        near, both, far = together((e[0], j3, x3), sum1, fourth)
        a0b2 = jnp.where(home, jnp.concatenate([near, both], 1), jnp.concatenate([both, far], 1))
        a0b2_next = step(a0b2)
        sum2 = adjoint_of(columns(a0b2, 1, 2), columns(a0b2_next, 1, 2))
        part2 = cross(after(sum2, part1))
        rest = jnp.concatenate([e[2], e[3][rows:]], 0)
        j5 = home_jump(after(rest, j3))
        near, both, far = together((e[1], j4, x4), sum2, part0)
        a1b3 = jnp.where(home, jnp.concatenate([near, both], 1), jnp.concatenate([both, far], 1))
        a1b3_next = step(a1b3)
        v_other = swap(after(value_next, sum1))
        sum3 = adjoint_of(columns(a1b3, 1, 2), columns(a1b3_next, 1, 2))
        part3 = cross(after(sum3, part2))

        def own_and_swapped(near, far):
            return jnp.where(mine, near, far), swap(jnp.where(mine, far, near))

        parts = together((x1, x2, x3, x4, v_across2, v_across3), sum1)
        v_across = jnp.concatenate(
            [jnp.where(home, parts[2], parts[0]), jnp.where(home, parts[3], parts[1]), parts[4], parts[5]], 1
        )
        v_across_other = swap(v_across)
        near, far = together((rest, j5), a1b3_next, part1)
        a_rest = jnp.where(home, near, far)
        a_rest_next = step(a_rest)
        b0, b0_next, b1, b1_next, a0b2, a0b2_next = together(
            (b0, b0_next, b1, b1_next, a0b2, a0b2_next), a1b3_next, sum3, part2, a_rest
        )
        a0, a0_next = columns(a0b2, 0, 1), columns(a0b2_next, 0, 1)
        a1, a1_next = columns(a1b3, 0, 1), columns(a1b3_next, 0, 1)
        b_own, b_swapped = own_and_swapped(
            jnp.concatenate([b0, b1, columns(a0b2, 1, 2), columns(a1b3, 1, 2)], 1),
            jnp.concatenate([b0_next, b1_next, columns(a0b2_next, 1, 2), columns(a1b3_next, 1, 2)], 1),
        )
        a01_own, a01_swapped = own_and_swapped(
            jnp.concatenate([a0, a1], 1), jnp.concatenate([a0_next, a1_next], 1)
        )
        grad = dott(
            jnp.concatenate([b_own, b_swapped], 1), jnp.concatenate([v_across, v_across_other], 1)
        ) + dott(
            jnp.concatenate([a01_own, a01_swapped], 1),
            jnp.concatenate([columns(value_next, 0, 2), columns(v_other, 0, 2)], 1),
        )
        own01 = adjoint_of(jnp.concatenate([a0, a1], 1), jnp.concatenate([a0_next, a1_next], 1))
        near, far, near_top, far_top = together((a_rest, a_rest_next, a3_top, a3_top_next), grad, own01)

        def two_quarters(rest, top):
            return jnp.concatenate([rest[: 2 * rows], jnp.concatenate([top, rest[2 * rows :]], 0)], 1)

        near, far = two_quarters(near, near_top), two_quarters(far, far_top)
        a23_own, a23_swapped = own_and_swapped(near, far)
        grad = df * (grad + dott(
            jnp.concatenate([a23_own, a23_swapped], 1),
            jnp.concatenate([columns(value_next, 2, 4), columns(v_other, 2, 4)], 1),
        ))
        own23 = adjoint_of(near, far)
        own23, part3, grad = together((own23, part3, grad))
        adjoint = df * (
            jnp.concatenate([own01, own23], 1) + jnp.concatenate([part0, part1, part2, part3], 1)
        )
        return adjoint, grad

    return shards


def solution(mesh):
    sizes = tuple(mesh.shape[a] for a in AXES)
    shards = two_side_shards(sizes) if sizes[1:] == (4, 2, 2) else plain_shards
    return jax.shard_map(
        shards,
        mesh=mesh,
        in_specs=(
            P(("groups", "markov"), ("storage", "sub")),
            P(("groups", "markov"), ("storage", "sub")),
            P(("groups", "storage", "sub"), "markov"),
            P("groups"),
        ),
        out_specs=(
            P(("groups", "markov"), ("storage", "sub")),
            P(("groups", "storage", "sub"), "markov"),
        ),
        check_vma=False,
    )
```

```python
import jax
import jax.numpy as jnp
from jax import lax
from jax.sharding import PartitionSpec as P

discount_rate = 0.97
AXES = ("groups", "markov", "storage", "sub")


def factor_of(section):
    return jnp.exp(section[0].astype(jnp.float32) * jnp.log(jnp.float32(discount_rate)))


def plain_shards(expected_cot, value_next, transition, section):
    discount_factor = factor_of(section)
    cotangent_all = lax.all_gather(expected_cot, "markov", axis=0, tiled=True)
    adjoint_sum = lax.dot_general(
        lax.all_gather(transition, ("storage", "sub"), axis=0, tiled=True),
        cotangent_all,
        (((0,), (0,)), ((), ())),
        preferred_element_type=jnp.float32,
    )
    own_states = lax.all_to_all(
        cotangent_all, ("storage", "sub"), split_axis=0, concat_axis=1, tiled=True
    )
    gathered_values = lax.all_gather(value_next, ("storage", "sub"), axis=1, tiled=True)
    gradient_sum = lax.dot_general(
        own_states, gathered_values, (((1,), (1,)), ((), ())), preferred_element_type=jnp.float32
    )
    return (discount_factor * adjoint_sum, discount_factor * gradient_sum)


def tdot(a, b):
    return lax.dot_general(a, b, (((0,), (0,)), ((), ())), preferred_element_type=jnp.float32)


def dott(a, b):
    return lax.dot_general(a, b, (((1,), (1,)), ((), ())), preferred_element_type=jnp.float32)


def after(array, *others):
    return lax.optimization_barrier((array,) + others)[0]


def two_side_shards(sizes):
    groups, layers, sides, cores = sizes
    places = [(g, z, s, c) for g in range(groups) for z in range(layers) for s in range(sides) for c in range(cores)]
    index = {place: i for i, place in enumerate(places)}

    def pairs(move, chosen=lambda g, z, s, c: True):
        return [(index[p], index[move(*p)]) for p in places if chosen(*p)]

    def is_home(g, z, s, c):
        return z // 2 == s

    def jumped(g, z, s, c):
        return (g, z ^ 2, s, c)

    cross_pairs = pairs(lambda g, z, s, c: (g, z, 1 - s, c))
    step_pairs = pairs(lambda g, z, s, c: (g, z ^ 1, s, c))
    core_pairs = pairs(lambda g, z, s, c: (g, z, s, 1 - c))
    jump_pairs, home_jump_pairs = pairs(jumped), pairs(jumped, is_home)

    def cross(a):
        return lax.ppermute(a, AXES, cross_pairs)

    def step(a):
        return lax.ppermute(a, AXES, step_pairs)

    def swap(a):
        return lax.ppermute(a, AXES, core_pairs)

    def home_jump(a):
        return lax.ppermute(a, AXES, home_jump_pairs)

    def jump(a):
        return lax.ppermute(a, AXES, jump_pairs)

    def shards(expected_cot, value_next, transition, section):
        df = factor_of(section)
        z, s, c = lax.axis_index("markov"), lax.axis_index("storage"), lax.axis_index("sub")
        home = z // 2 == s
        mine = z % 2 == c
        half = expected_cot.shape[1] // 2
        quarter = half // 2

        def columns(array, start, stop):
            return array[:, start * quarter : stop * quarter]

        def together(arrays, *gates):
            return lax.optimization_barrier(tuple(arrays) + gates)[: len(arrays)]

        e = [columns(expected_cot, i, i + 1) for i in range(4)]
        v = [columns(value_next, i, i + 1) for i in range(4)]
        rows = e[3].shape[0] // 2
        early_rows = after(e[3][:rows])
        j0 = home_jump(early_rows)
        value_next, expected_cot = together((value_next, expected_cot), early_rows)
        e = [columns(expected_cot, i, i + 1) for i in range(4)]
        v = [columns(value_next, i, i + 1) for i in range(4)]
        x1 = cross(jnp.where(home, v[0], e[0]))
        t_other = swap(transition)
        e2 = after(e[2], x1)
        j1 = jump(jnp.where(home, x1, e2))
        t_near, t_next = jnp.where(mine, transition, t_other), jnp.where(mine, t_other, transition)

        def adjoint_of(near, far):
            return tdot(t_near, near) + tdot(t_next, far)

        v1, e1 = together((v[1], e[1]), x1, t_near, j0)
        x2 = cross(jnp.concatenate([jnp.where(home, v1, e1), v[2]], 1))
        x2, v_across2 = columns(x2, 0, 1), columns(x2, 1, 2)
        near, far = together((e[3][:rows], j0), x1)
        a3_top = jnp.where(home, near, far)
        a3_top_next = step(a3_top)
        second = jnp.where(home, x2, e[3])
        j2 = jump(second)
        near, far = together((j1, v[0]), second)
        third_cross = jnp.where(home, near, far)
        x3 = cross(jnp.concatenate([third_cross, v[3]], 1))
        x3, v_across3 = columns(x3, 0, 1), columns(x3, 1, 2)
        near, far = together((x1, j1), third_cross, a3_top_next)
        b0 = jnp.where(home, near, far)
        b0_next = step(b0)
        third = jnp.where(home, e[0], x3)
        j3 = jump(third)
        sum0 = adjoint_of(b0, b0_next)
        near, far = together((j2, v[1]), third)
        x4 = cross(jnp.where(home, near, far))
        near, far = together((x2, j2), sum0, third)
        b1 = jnp.where(home, near, far)
        b1_next = step(b1)
        part0 = cross(after(sum0, x4))
        fourth = jnp.where(home, e[1], x4)
        j4 = jump(fourth)
        sum1 = adjoint_of(b1, b1_next)
        part1 = cross(after(sum1, part0))
        near, both, far = together((e[0], j3, x3), sum1, fourth)
        a0b2 = jnp.where(home, jnp.concatenate([near, both], 1), jnp.concatenate([both, far], 1))
        a0b2_next = step(a0b2)
        sum2 = adjoint_of(columns(a0b2, 1, 2), columns(a0b2_next, 1, 2))
        part2 = cross(after(sum2, part1))
        rest = jnp.concatenate([e[2], e[3][rows:]], 0)
        j5 = home_jump(after(rest, j3))
        near, both, far = together((e[1], j4, x4), sum2, part0)
        a1b3 = jnp.where(home, jnp.concatenate([near, both], 1), jnp.concatenate([both, far], 1))
        a1b3_next = step(a1b3)
        v_other = swap(after(value_next, sum1))
        sum3 = adjoint_of(columns(a1b3, 1, 2), columns(a1b3_next, 1, 2))
        part3 = cross(after(sum3, part2))

        def own_and_swapped(near, far):
            return jnp.where(mine, near, far), swap(jnp.where(mine, far, near))

        parts = together((x1, x2, x3, x4, v_across2, v_across3), sum1)
        v_across = jnp.concatenate(
            [jnp.where(home, parts[2], parts[0]), jnp.where(home, parts[3], parts[1]), parts[4], parts[5]], 1
        )
        v_across_other = swap(v_across)
        near, far = together((rest, j5), a1b3_next, part1)
        a_rest = jnp.where(home, near, far)
        a_rest_next = step(a_rest)
        b0, b0_next, b1, b1_next, a0b2, a0b2_next = together(
            (b0, b0_next, b1, b1_next, a0b2, a0b2_next), a1b3_next, sum3, part2, a_rest
        )
        a0, a0_next = columns(a0b2, 0, 1), columns(a0b2_next, 0, 1)
        a1, a1_next = columns(a1b3, 0, 1), columns(a1b3_next, 0, 1)
        b_own, b_swapped = own_and_swapped(
            jnp.concatenate([b0, b1, columns(a0b2, 1, 2), columns(a1b3, 1, 2)], 1),
            jnp.concatenate([b0_next, b1_next, columns(a0b2_next, 1, 2), columns(a1b3_next, 1, 2)], 1),
        )
        a01_own, a01_swapped = own_and_swapped(
            jnp.concatenate([a0, a1], 1), jnp.concatenate([a0_next, a1_next], 1)
        )
        grad = dott(
            jnp.concatenate([b_own, b_swapped], 1), jnp.concatenate([v_across, v_across_other], 1)
        ) + dott(
            jnp.concatenate([a01_own, a01_swapped], 1),
            jnp.concatenate([columns(value_next, 0, 2), columns(v_other, 0, 2)], 1),
        )
        own01 = adjoint_of(jnp.concatenate([a0, a1], 1), jnp.concatenate([a0_next, a1_next], 1))
        near, far, near_top, far_top = together((a_rest, a_rest_next, a3_top, a3_top_next), grad, own01)

        def two_quarters(rest, top):
            return jnp.concatenate([rest[: 2 * rows], jnp.concatenate([top, rest[2 * rows :]], 0)], 1)

        near, far = two_quarters(near, near_top), two_quarters(far, far_top)
        a23_own, a23_swapped = own_and_swapped(near, far)
        grad = df * (grad + dott(
            jnp.concatenate([a23_own, a23_swapped], 1),
            jnp.concatenate([columns(value_next, 2, 4), columns(v_other, 2, 4)], 1),
        ))
        own23 = adjoint_of(near, far)
        own23, part3, grad = together((own23, part3, grad))
        adjoint = df * (
            jnp.concatenate([own01, own23], 1) + jnp.concatenate([part0, part1, part2, part3], 1)
        )
        return adjoint, grad

    return shards


def solution(mesh):
    sizes = tuple(mesh.shape[a] for a in AXES)
    shards = two_side_shards(sizes) if sizes[1:] == (4, 2, 2) else plain_shards
    return jax.shard_map(
        shards,
        mesh=mesh,
        in_specs=(
            P(("groups", "markov"), ("storage", "sub")),
            P(("groups", "markov"), ("storage", "sub")),
            P(("groups", "storage", "sub"), "markov"),
            P("groups"),
        ),
        out_specs=(
            P(("groups", "markov"), ("storage", "sub")),
            P(("groups", "storage", "sub"), "markov"),
        ),
        check_vma=False,
    )
```

```python
import jax
import jax.numpy as jnp
from jax import lax
from jax.sharding import PartitionSpec as P

discount_rate = 0.97
AXES = ("groups", "markov", "storage", "sub")


def factor_of(section):
    return jnp.exp(section[0].astype(jnp.float32) * jnp.log(jnp.float32(discount_rate)))


def plain_shards(expected_cot, value_next, transition, section):
    discount_factor = factor_of(section)
    cotangent_all = lax.all_gather(expected_cot, "markov", axis=0, tiled=True)
    adjoint_sum = lax.dot_general(
        lax.all_gather(transition, ("storage", "sub"), axis=0, tiled=True),
        cotangent_all,
        (((0,), (0,)), ((), ())),
        preferred_element_type=jnp.float32,
    )
    own_states = lax.all_to_all(
        cotangent_all, ("storage", "sub"), split_axis=0, concat_axis=1, tiled=True
    )
    gathered_values = lax.all_gather(value_next, ("storage", "sub"), axis=1, tiled=True)
    gradient_sum = lax.dot_general(
        own_states, gathered_values, (((1,), (1,)), ((), ())), preferred_element_type=jnp.float32
    )
    return (discount_factor * adjoint_sum, discount_factor * gradient_sum)


def tdot(a, b):
    return lax.dot_general(a, b, (((0,), (0,)), ((), ())), preferred_element_type=jnp.float32)


def dott(a, b):
    return lax.dot_general(a, b, (((1,), (1,)), ((), ())), preferred_element_type=jnp.float32)


def after(array, *others):
    return lax.optimization_barrier((array,) + others)[0]


def two_side_shards(sizes):
    groups, layers, sides, cores = sizes
    places = [(g, z, s, c) for g in range(groups) for z in range(layers) for s in range(sides) for c in range(cores)]
    index = {place: i for i, place in enumerate(places)}

    def pairs(move, chosen=lambda g, z, s, c: True):
        return [(index[p], index[move(*p)]) for p in places if chosen(*p)]

    def is_home(g, z, s, c):
        return z // 2 == s

    def jumped(g, z, s, c):
        return (g, z ^ 2, s, c)

    cross_pairs = pairs(lambda g, z, s, c: (g, z, 1 - s, c))
    step_pairs = pairs(lambda g, z, s, c: (g, z ^ 1, s, c))
    core_pairs = pairs(lambda g, z, s, c: (g, z, s, 1 - c))
    jump_pairs, home_jump_pairs = pairs(jumped), pairs(jumped, is_home)

    def cross(a):
        return lax.ppermute(a, AXES, cross_pairs)

    def step(a):
        return lax.ppermute(a, AXES, step_pairs)

    def swap(a):
        return lax.ppermute(a, AXES, core_pairs)

    def home_jump(a):
        return lax.ppermute(a, AXES, home_jump_pairs)

    def jump(a):
        return lax.ppermute(a, AXES, jump_pairs)

    def shards(expected_cot, value_next, transition, section):
        df = factor_of(section)
        z, s, c = lax.axis_index("markov"), lax.axis_index("storage"), lax.axis_index("sub")
        home = z // 2 == s
        mine = z % 2 == c
        half = expected_cot.shape[1] // 2
        quarter = half // 2

        def columns(array, start, stop):
            return array[:, start * quarter : stop * quarter]

        def together(arrays, *gates):
            return lax.optimization_barrier(tuple(arrays) + gates)[: len(arrays)]

        e = [columns(expected_cot, i, i + 1) for i in range(4)]
        v = [columns(value_next, i, i + 1) for i in range(4)]
        x1 = cross(jnp.where(home, v[0], e[0]))
        height = e[3].shape[0]
        rows = height // 4
        j0 = home_jump(e[3][:rows])
        t_other = swap(transition)
        e2 = after(e[2], x1)
        j1 = jump(jnp.where(home, x1, e2))
        t_near, t_next = jnp.where(mine, transition, t_other), jnp.where(mine, t_other, transition)

        def adjoint_of(near, far):
            return tdot(t_near, near) + tdot(t_next, far)

        v1, e1 = together((v[1], e[1]), x1, t_near, j0)
        x2 = cross(jnp.concatenate([jnp.where(home, v1, e1), v[2]], 1))
        x2, v_across2 = columns(x2, 0, 1), columns(x2, 1, 2)
        near, far = together((e[3][:rows], j0), x1)
        a3_top = jnp.where(home, near, far)
        a3_top_next = step(a3_top)
        second = jnp.where(home, x2, e[3])
        j2 = jump(second)
        near, far = together((j1, v[0]), second)
        third_cross = jnp.where(home, near, far)
        x3 = cross(jnp.concatenate([third_cross, v[3]], 1))
        x3, v_across3 = columns(x3, 0, 1), columns(x3, 1, 2)
        near, far = together((x1, j1), third_cross, a3_top_next)
        b0 = jnp.where(home, near, far)
        b0_next = step(b0)
        third = jnp.where(home, e[0], x3)
        j3 = jump(third)
        sum0 = adjoint_of(b0, b0_next)
        near, far = together((j2, v[1]), third)
        x4 = cross(jnp.where(home, near, far))
        near, far = together((x2, j2), sum0, third)
        b1 = jnp.where(home, near, far)
        b1_next = step(b1)
        part0 = cross(after(sum0, x4))
        fourth = jnp.where(home, e[1], x4)
        j4 = jump(fourth)
        sum1 = adjoint_of(b1, b1_next)
        part1 = cross(after(sum1, part0))
        near, both, far = together((e[0], j3, x3), sum1, fourth)
        a0b2 = jnp.where(home, jnp.concatenate([near, both], 1), jnp.concatenate([both, far], 1))
        a0b2_next = step(a0b2)
        sum2 = adjoint_of(columns(a0b2, 1, 2), columns(a0b2_next, 1, 2))
        part2 = cross(after(sum2, part1))
        rest = jnp.concatenate([e[2], e[3][rows:]], 0)
        j5 = home_jump(after(rest, j3))
        near, both, far = together((e[1], j4, x4), sum2, part0)
        a1b3 = jnp.where(home, jnp.concatenate([near, both], 1), jnp.concatenate([both, far], 1))
        a1b3_next = step(a1b3)
        v_other = swap(after(value_next, sum1))
        sum3 = adjoint_of(columns(a1b3, 1, 2), columns(a1b3_next, 1, 2))
        part3 = cross(after(sum3, part2))

        def own_and_swapped(near, far):
            return jnp.where(mine, near, far), swap(jnp.where(mine, far, near))

        parts = together((x1, x2, x3, x4, v_across2, v_across3), sum1)
        v_across = jnp.concatenate(
            [jnp.where(home, parts[2], parts[0]), jnp.where(home, parts[3], parts[1]), parts[4], parts[5]], 1
        )
        v_across_other = swap(v_across)
        near, far = together((rest, j5), a1b3_next, part1)
        a_rest = jnp.where(home, near, far)
        a_rest_next = step(a_rest)
        b0, b0_next, b1, b1_next, a0b2, a0b2_next = together(
            (b0, b0_next, b1, b1_next, a0b2, a0b2_next), a1b3_next, sum3, part2, a_rest
        )
        a0, a0_next = columns(a0b2, 0, 1), columns(a0b2_next, 0, 1)
        a1, a1_next = columns(a1b3, 0, 1), columns(a1b3_next, 0, 1)
        b_own, b_swapped = own_and_swapped(
            jnp.concatenate([b0, b1, columns(a0b2, 1, 2), columns(a1b3, 1, 2)], 1),
            jnp.concatenate([b0_next, b1_next, columns(a0b2_next, 1, 2), columns(a1b3_next, 1, 2)], 1),
        )
        a01_own, a01_swapped = own_and_swapped(
            jnp.concatenate([a0, a1], 1), jnp.concatenate([a0_next, a1_next], 1)
        )
        grad = dott(
            jnp.concatenate([b_own, b_swapped], 1), jnp.concatenate([v_across, v_across_other], 1)
        ) + dott(
            jnp.concatenate([a01_own, a01_swapped], 1),
            jnp.concatenate([columns(value_next, 0, 2), columns(v_other, 0, 2)], 1),
        )
        own01 = adjoint_of(jnp.concatenate([a0, a1], 1), jnp.concatenate([a0_next, a1_next], 1))
        near, far, near_top, far_top = together((a_rest, a_rest_next, a3_top, a3_top_next), grad, own01)

        def two_quarters(rest, top):
            return jnp.concatenate([rest[:height], jnp.concatenate([top, rest[height:]], 0)], 1)

        near, far = two_quarters(near, near_top), two_quarters(far, far_top)
        a23_own, a23_swapped = own_and_swapped(near, far)
        grad = df * (grad + dott(
            jnp.concatenate([a23_own, a23_swapped], 1),
            jnp.concatenate([columns(value_next, 2, 4), columns(v_other, 2, 4)], 1),
        ))
        own23 = adjoint_of(near, far)
        own23, part3, grad = together((own23, part3, grad))
        adjoint = df * (
            jnp.concatenate([own01, own23], 1) + jnp.concatenate([part0, part1, part2, part3], 1)
        )
        return adjoint, grad

    return shards


def solution(mesh):
    sizes = tuple(mesh.shape[a] for a in AXES)
    shards = two_side_shards(sizes) if sizes[1:] == (4, 2, 2) else plain_shards
    return jax.shard_map(
        shards,
        mesh=mesh,
        in_specs=(
            P(("groups", "markov"), ("storage", "sub")),
            P(("groups", "markov"), ("storage", "sub")),
            P(("groups", "storage", "sub"), "markov"),
            P("groups"),
        ),
        out_specs=(
            P(("groups", "markov"), ("storage", "sub")),
            P(("groups", "storage", "sub"), "markov"),
        ),
        check_vma=False,
    )
```

```python
import jax
import jax.numpy as jnp
from jax import lax
from jax.sharding import PartitionSpec as P

discount_rate = 0.97
AXES = ("groups", "markov", "storage", "sub")


def factor_of(section):
    return jnp.exp(section[0].astype(jnp.float32) * jnp.log(jnp.float32(discount_rate)))


def plain_shards(expected_cot, value_next, transition, section):
    discount_factor = factor_of(section)
    cotangent_all = lax.all_gather(expected_cot, "markov", axis=0, tiled=True)
    adjoint_sum = lax.dot_general(
        lax.all_gather(transition, ("storage", "sub"), axis=0, tiled=True),
        cotangent_all,
        (((0,), (0,)), ((), ())),
        preferred_element_type=jnp.float32,
    )
    own_states = lax.all_to_all(
        cotangent_all, ("storage", "sub"), split_axis=0, concat_axis=1, tiled=True
    )
    gathered_values = lax.all_gather(value_next, ("storage", "sub"), axis=1, tiled=True)
    gradient_sum = lax.dot_general(
        own_states, gathered_values, (((1,), (1,)), ((), ())), preferred_element_type=jnp.float32
    )
    return (discount_factor * adjoint_sum, discount_factor * gradient_sum)


def tdot(a, b):
    return lax.dot_general(a, b, (((0,), (0,)), ((), ())), preferred_element_type=jnp.float32)


def dott(a, b):
    return lax.dot_general(a, b, (((1,), (1,)), ((), ())), preferred_element_type=jnp.float32)


def after(array, *others):
    return lax.optimization_barrier((array,) + others)[0]


def two_side_shards(sizes):
    groups, layers, sides, cores = sizes
    places = [(g, z, s, c) for g in range(groups) for z in range(layers) for s in range(sides) for c in range(cores)]
    index = {place: i for i, place in enumerate(places)}

    def pairs(move, chosen=lambda g, z, s, c: True):
        return [(index[p], index[move(*p)]) for p in places if chosen(*p)]

    def is_home(g, z, s, c):
        return z // 2 == s

    def jumped(g, z, s, c):
        return (g, z ^ 2, s, c)

    cross_pairs = pairs(lambda g, z, s, c: (g, z, 1 - s, c))
    step_pairs = pairs(lambda g, z, s, c: (g, z ^ 1, s, c))
    core_pairs = pairs(lambda g, z, s, c: (g, z, s, 1 - c))
    jump_pairs, home_jump_pairs = pairs(jumped), pairs(jumped, is_home)

    def cross(a):
        return lax.ppermute(a, AXES, cross_pairs)

    def step(a):
        return lax.ppermute(a, AXES, step_pairs)

    def swap(a):
        return lax.ppermute(a, AXES, core_pairs)

    def home_jump(a):
        return lax.ppermute(a, AXES, home_jump_pairs)

    def jump(a):
        return lax.ppermute(a, AXES, jump_pairs)

    def shards(expected_cot, value_next, transition, section):
        df = factor_of(section)
        z, s, c = lax.axis_index("markov"), lax.axis_index("storage"), lax.axis_index("sub")
        home = z // 2 == s
        mine = z % 2 == c
        half = expected_cot.shape[1] // 2
        quarter = half // 2

        def columns(array, start, stop):
            return array[:, start * quarter : stop * quarter]

        def together(arrays, *gates):
            return lax.optimization_barrier(tuple(arrays) + gates)[: len(arrays)]

        e = [columns(expected_cot, i, i + 1) for i in range(4)]
        v = [columns(value_next, i, i + 1) for i in range(4)]
        x1 = cross(jnp.where(home, v[0], e[0]))
        height = e[3].shape[0]
        rows = height * 3 // 4
        j0 = home_jump(e[3][:rows])
        t_other = swap(transition)
        e2 = after(e[2], x1)
        j1 = jump(jnp.where(home, x1, e2))
        t_near, t_next = jnp.where(mine, transition, t_other), jnp.where(mine, t_other, transition)

        def adjoint_of(near, far):
            return tdot(t_near, near) + tdot(t_next, far)

        v1, e1 = together((v[1], e[1]), x1, t_near, j0)
        x2 = cross(jnp.concatenate([jnp.where(home, v1, e1), v[2]], 1))
        x2, v_across2 = columns(x2, 0, 1), columns(x2, 1, 2)
        near, far = together((e[3][:rows], j0), x1)
        a3_top = jnp.where(home, near, far)
        a3_top_next = step(a3_top)
        second = jnp.where(home, x2, e[3])
        j2 = jump(second)
        near, far = together((j1, v[0]), second)
        third_cross = jnp.where(home, near, far)
        x3 = cross(jnp.concatenate([third_cross, v[3]], 1))
        x3, v_across3 = columns(x3, 0, 1), columns(x3, 1, 2)
        near, far = together((x1, j1), third_cross, a3_top_next)
        b0 = jnp.where(home, near, far)
        b0_next = step(b0)
        third = jnp.where(home, e[0], x3)
        j3 = jump(third)
        sum0 = adjoint_of(b0, b0_next)
        near, far = together((j2, v[1]), third)
        x4 = cross(jnp.where(home, near, far))
        near, far = together((x2, j2), sum0, third)
        b1 = jnp.where(home, near, far)
        b1_next = step(b1)
        part0 = cross(after(sum0, x4))
        fourth = jnp.where(home, e[1], x4)
        j4 = jump(fourth)
        sum1 = adjoint_of(b1, b1_next)
        part1 = cross(after(sum1, part0))
        near, both, far = together((e[0], j3, x3), sum1, fourth)
        a0b2 = jnp.where(home, jnp.concatenate([near, both], 1), jnp.concatenate([both, far], 1))
        a0b2_next = step(a0b2)
        sum2 = adjoint_of(columns(a0b2, 1, 2), columns(a0b2_next, 1, 2))
        part2 = cross(after(sum2, part1))
        rest = jnp.concatenate([e[2], e[3][rows:]], 0)
        j5 = home_jump(after(rest, j3))
        near, both, far = together((e[1], j4, x4), sum2, part0)
        a1b3 = jnp.where(home, jnp.concatenate([near, both], 1), jnp.concatenate([both, far], 1))
        a1b3_next = step(a1b3)
        v_other = swap(after(value_next, sum1))
        sum3 = adjoint_of(columns(a1b3, 1, 2), columns(a1b3_next, 1, 2))
        part3 = cross(after(sum3, part2))

        def own_and_swapped(near, far):
            return jnp.where(mine, near, far), swap(jnp.where(mine, far, near))

        parts = together((x1, x2, x3, x4, v_across2, v_across3), sum1)
        v_across = jnp.concatenate(
            [jnp.where(home, parts[2], parts[0]), jnp.where(home, parts[3], parts[1]), parts[4], parts[5]], 1
        )
        v_across_other = swap(v_across)
        near, far = together((rest, j5), a1b3_next, part1)
        a_rest = jnp.where(home, near, far)
        a_rest_next = step(a_rest)
        b0, b0_next, b1, b1_next, a0b2, a0b2_next = together(
            (b0, b0_next, b1, b1_next, a0b2, a0b2_next), a1b3_next, sum3, part2, a_rest
        )
        a0, a0_next = columns(a0b2, 0, 1), columns(a0b2_next, 0, 1)
        a1, a1_next = columns(a1b3, 0, 1), columns(a1b3_next, 0, 1)
        b_own, b_swapped = own_and_swapped(
            jnp.concatenate([b0, b1, columns(a0b2, 1, 2), columns(a1b3, 1, 2)], 1),
            jnp.concatenate([b0_next, b1_next, columns(a0b2_next, 1, 2), columns(a1b3_next, 1, 2)], 1),
        )
        a01_own, a01_swapped = own_and_swapped(
            jnp.concatenate([a0, a1], 1), jnp.concatenate([a0_next, a1_next], 1)
        )
        grad = dott(
            jnp.concatenate([b_own, b_swapped], 1), jnp.concatenate([v_across, v_across_other], 1)
        ) + dott(
            jnp.concatenate([a01_own, a01_swapped], 1),
            jnp.concatenate([columns(value_next, 0, 2), columns(v_other, 0, 2)], 1),
        )
        own01 = adjoint_of(jnp.concatenate([a0, a1], 1), jnp.concatenate([a0_next, a1_next], 1))
        near, far, near_top, far_top = together((a_rest, a_rest_next, a3_top, a3_top_next), grad, own01)

        def two_quarters(rest, top):
            return jnp.concatenate([rest[:height], jnp.concatenate([top, rest[height:]], 0)], 1)

        near, far = two_quarters(near, near_top), two_quarters(far, far_top)
        a23_own, a23_swapped = own_and_swapped(near, far)
        grad = df * (grad + dott(
            jnp.concatenate([a23_own, a23_swapped], 1),
            jnp.concatenate([columns(value_next, 2, 4), columns(v_other, 2, 4)], 1),
        ))
        own23 = adjoint_of(near, far)
        own23, part3, grad = together((own23, part3, grad))
        adjoint = df * (
            jnp.concatenate([own01, own23], 1) + jnp.concatenate([part0, part1, part2, part3], 1)
        )
        return adjoint, grad

    return shards


def solution(mesh):
    sizes = tuple(mesh.shape[a] for a in AXES)
    shards = two_side_shards(sizes) if sizes[1:] == (4, 2, 2) else plain_shards
    return jax.shard_map(
        shards,
        mesh=mesh,
        in_specs=(
            P(("groups", "markov"), ("storage", "sub")),
            P(("groups", "markov"), ("storage", "sub")),
            P(("groups", "storage", "sub"), "markov"),
            P("groups"),
        ),
        out_specs=(
            P(("groups", "markov"), ("storage", "sub")),
            P(("groups", "storage", "sub"), "markov"),
        ),
        check_vma=False,
    )
```

```python
import jax
import jax.numpy as jnp
from jax import lax
from jax.sharding import PartitionSpec as P

discount_rate = 0.97
AXES = ("groups", "markov", "storage", "sub")


def factor_of(section):
    return jnp.exp(section[0].astype(jnp.float32) * jnp.log(jnp.float32(discount_rate)))


def plain_shards(expected_cot, value_next, transition, section):
    discount_factor = factor_of(section)
    cotangent_all = lax.all_gather(expected_cot, "markov", axis=0, tiled=True)
    adjoint_sum = lax.dot_general(
        lax.all_gather(transition, ("storage", "sub"), axis=0, tiled=True),
        cotangent_all,
        (((0,), (0,)), ((), ())),
        preferred_element_type=jnp.float32,
    )
    own_states = lax.all_to_all(
        cotangent_all, ("storage", "sub"), split_axis=0, concat_axis=1, tiled=True
    )
    gathered_values = lax.all_gather(value_next, ("storage", "sub"), axis=1, tiled=True)
    gradient_sum = lax.dot_general(
        own_states, gathered_values, (((1,), (1,)), ((), ())), preferred_element_type=jnp.float32
    )
    return (discount_factor * adjoint_sum, discount_factor * gradient_sum)


def tdot(a, b):
    return lax.dot_general(a, b, (((0,), (0,)), ((), ())), preferred_element_type=jnp.float32)


def dott(a, b):
    return lax.dot_general(a, b, (((1,), (1,)), ((), ())), preferred_element_type=jnp.float32)


def after(array, *others):
    return lax.optimization_barrier((array,) + others)[0]


def two_side_shards(sizes):
    groups, layers, sides, cores = sizes
    places = [(g, z, s, c) for g in range(groups) for z in range(layers) for s in range(sides) for c in range(cores)]
    index = {place: i for i, place in enumerate(places)}

    def pairs(move, chosen=lambda g, z, s, c: True):
        return [(index[p], index[move(*p)]) for p in places if chosen(*p)]

    def is_home(g, z, s, c):
        return z // 2 == s

    def jumped(g, z, s, c):
        return (g, z ^ 2, s, c)

    cross_pairs = pairs(lambda g, z, s, c: (g, z, 1 - s, c))
    step_pairs = pairs(lambda g, z, s, c: (g, z ^ 1, s, c))
    core_pairs = pairs(lambda g, z, s, c: (g, z, s, 1 - c))
    jump_pairs, home_jump_pairs = pairs(jumped), pairs(jumped, is_home)

    def cross(a):
        return lax.ppermute(a, AXES, cross_pairs)

    def step(a):
        return lax.ppermute(a, AXES, step_pairs)

    def swap(a):
        return lax.ppermute(a, AXES, core_pairs)

    def home_jump(a):
        return lax.ppermute(a, AXES, home_jump_pairs)

    def jump(a):
        return lax.ppermute(a, AXES, jump_pairs)

    def shards(expected_cot, value_next, transition, section):
        df = factor_of(section)
        z, s, c = lax.axis_index("markov"), lax.axis_index("storage"), lax.axis_index("sub")
        home = z // 2 == s
        mine = z % 2 == c
        half = expected_cot.shape[1] // 2
        quarter = half // 2

        def columns(array, start, stop):
            return array[:, start * quarter : stop * quarter]

        def together(arrays, *gates):
            return lax.optimization_barrier(tuple(arrays) + gates)[: len(arrays)]

        e = [columns(expected_cot, i, i + 1) for i in range(4)]
        v = [columns(value_next, i, i + 1) for i in range(4)]
        x1 = cross(jnp.where(home, v[0], e[0]))
        rows = e[3].shape[0] // 2
        j0 = home_jump(e[3][:rows])
        t_other = swap(transition)
        e2 = after(e[2], x1, j0)
        j1 = jump(jnp.where(home, x1, e2))
        t_near, t_next = jnp.where(mine, transition, t_other), jnp.where(mine, t_other, transition)

        def adjoint_of(near, far):
            return tdot(t_near, near) + tdot(t_next, far)

        v1, e1 = together((v[1], e[1]), x1, t_near)
        x2 = cross(jnp.concatenate([jnp.where(home, v1, e1), v[2]], 1))
        x2, v_across2 = columns(x2, 0, 1), columns(x2, 1, 2)
        near, far = together((e[3][:rows], j0), x1)
        a3_top = jnp.where(home, near, far)
        a3_top_next = step(a3_top)
        second = jnp.where(home, x2, e[3])
        j2 = jump(second)
        near, far = together((j1, v[0]), second)
        third_cross = jnp.where(home, near, far)
        x3 = cross(jnp.concatenate([third_cross, v[3]], 1))
        x3, v_across3 = columns(x3, 0, 1), columns(x3, 1, 2)
        near, far = together((x1, j1), third_cross, a3_top_next)
        b0 = jnp.where(home, near, far)
        b0_next = step(b0)
        third = jnp.where(home, e[0], x3)
        j3 = jump(third)
        sum0 = adjoint_of(b0, b0_next)
        near, far = together((j2, v[1]), third)
        x4 = cross(jnp.where(home, near, far))
        near, far = together((x2, j2), sum0, third)
        b1 = jnp.where(home, near, far)
        b1_next = step(b1)
        part0 = cross(after(sum0, x4))
        fourth = jnp.where(home, e[1], x4)
        j4 = jump(fourth)
        sum1 = adjoint_of(b1, b1_next)
        part1 = cross(after(sum1, part0))
        near, both, far = together((e[0], j3, x3), sum1, fourth)
        a0b2 = jnp.where(home, jnp.concatenate([near, both], 1), jnp.concatenate([both, far], 1))
        a0b2_next = step(a0b2)
        sum2 = adjoint_of(columns(a0b2, 1, 2), columns(a0b2_next, 1, 2))
        part2 = cross(after(sum2, part1))
        rest = jnp.concatenate([e[2], e[3][rows:]], 0)
        j5 = home_jump(after(rest, j3))
        near, both, far = together((e[1], j4, x4), sum2, part0)
        a1b3 = jnp.where(home, jnp.concatenate([near, both], 1), jnp.concatenate([both, far], 1))
        a1b3_next = step(a1b3)
        v_other = swap(after(value_next, sum1))
        sum3 = adjoint_of(columns(a1b3, 1, 2), columns(a1b3_next, 1, 2))
        part3 = cross(after(sum3, part2))

        def own_and_swapped(near, far):
            return jnp.where(mine, near, far), swap(jnp.where(mine, far, near))

        parts = together((x1, x2, x3, x4, v_across2, v_across3), sum1)
        v_across = jnp.concatenate(
            [jnp.where(home, parts[2], parts[0]), jnp.where(home, parts[3], parts[1]), parts[4], parts[5]], 1
        )
        v_across_other = swap(v_across)
        near, far = together((rest, j5), a1b3_next, part1)
        a_rest = jnp.where(home, near, far)
        a_rest_next = step(a_rest)
        b0, b0_next, b1, b1_next, a0b2, a0b2_next = together(
            (b0, b0_next, b1, b1_next, a0b2, a0b2_next), a1b3_next, sum3, part2, a_rest
        )
        a0, a0_next = columns(a0b2, 0, 1), columns(a0b2_next, 0, 1)
        a1, a1_next = columns(a1b3, 0, 1), columns(a1b3_next, 0, 1)
        b_own, b_swapped = own_and_swapped(
            jnp.concatenate([b0, b1, columns(a0b2, 1, 2), columns(a1b3, 1, 2)], 1),
            jnp.concatenate([b0_next, b1_next, columns(a0b2_next, 1, 2), columns(a1b3_next, 1, 2)], 1),
        )
        a01_own, a01_swapped = own_and_swapped(
            jnp.concatenate([a0, a1], 1), jnp.concatenate([a0_next, a1_next], 1)
        )
        grad = dott(
            jnp.concatenate([b_own, b_swapped], 1), jnp.concatenate([v_across, v_across_other], 1)
        ) + dott(
            jnp.concatenate([a01_own, a01_swapped], 1),
            jnp.concatenate([columns(value_next, 0, 2), columns(v_other, 0, 2)], 1),
        )
        own01 = adjoint_of(jnp.concatenate([a0, a1], 1), jnp.concatenate([a0_next, a1_next], 1))
        near, far, near_top, far_top = together((a_rest, a_rest_next, a3_top, a3_top_next), grad, own01)

        def two_quarters(rest, top):
            return jnp.concatenate([rest[: 2 * rows], jnp.concatenate([top, rest[2 * rows :]], 0)], 1)

        near, far = two_quarters(near, near_top), two_quarters(far, far_top)
        a23_own, a23_swapped = own_and_swapped(near, far)
        grad = df * (grad + dott(
            jnp.concatenate([a23_own, a23_swapped], 1),
            jnp.concatenate([columns(value_next, 2, 4), columns(v_other, 2, 4)], 1),
        ))
        own23 = adjoint_of(near, far)
        own23, part3, grad = together((own23, part3, grad))
        adjoint = df * (
            jnp.concatenate([own01, own23], 1) + jnp.concatenate([part0, part1, part2, part3], 1)
        )
        return adjoint, grad

    return shards


def solution(mesh):
    sizes = tuple(mesh.shape[a] for a in AXES)
    shards = two_side_shards(sizes) if sizes[1:] == (4, 2, 2) else plain_shards
    return jax.shard_map(
        shards,
        mesh=mesh,
        in_specs=(
            P(("groups", "markov"), ("storage", "sub")),
            P(("groups", "markov"), ("storage", "sub")),
            P(("groups", "storage", "sub"), "markov"),
            P("groups"),
        ),
        out_specs=(
            P(("groups", "markov"), ("storage", "sub")),
            P(("groups", "storage", "sub"), "markov"),
        ),
        check_vma=False,
    )
```

```python
import jax
import jax.numpy as jnp
from jax import lax
from jax.sharding import PartitionSpec as P

discount_rate = 0.97
AXES = ("groups", "markov", "storage", "sub")


def factor_of(section):
    return jnp.exp(section[0].astype(jnp.float32) * jnp.log(jnp.float32(discount_rate)))


def plain_shards(expected_cot, value_next, transition, section):
    discount_factor = factor_of(section)
    cotangent_all = lax.all_gather(expected_cot, "markov", axis=0, tiled=True)
    adjoint_sum = lax.dot_general(
        lax.all_gather(transition, ("storage", "sub"), axis=0, tiled=True),
        cotangent_all,
        (((0,), (0,)), ((), ())),
        preferred_element_type=jnp.float32,
    )
    own_states = lax.all_to_all(
        cotangent_all, ("storage", "sub"), split_axis=0, concat_axis=1, tiled=True
    )
    gathered_values = lax.all_gather(value_next, ("storage", "sub"), axis=1, tiled=True)
    gradient_sum = lax.dot_general(
        own_states, gathered_values, (((1,), (1,)), ((), ())), preferred_element_type=jnp.float32
    )
    return (discount_factor * adjoint_sum, discount_factor * gradient_sum)


def tdot(a, b):
    return lax.dot_general(a, b, (((0,), (0,)), ((), ())), preferred_element_type=jnp.float32)


def dott(a, b):
    return lax.dot_general(a, b, (((1,), (1,)), ((), ())), preferred_element_type=jnp.float32)


def after(array, *others):
    return lax.optimization_barrier((array,) + others)[0]


def two_side_shards(sizes):
    groups, layers, sides, cores = sizes
    places = [(g, z, s, c) for g in range(groups) for z in range(layers) for s in range(sides) for c in range(cores)]
    index = {place: i for i, place in enumerate(places)}

    def pairs(move, chosen=lambda g, z, s, c: True):
        return [(index[p], index[move(*p)]) for p in places if chosen(*p)]

    def is_home(g, z, s, c):
        return z // 2 == s

    def jumped(g, z, s, c):
        return (g, z ^ 2, s, c)

    cross_pairs = pairs(lambda g, z, s, c: (g, z, 1 - s, c))
    step_pairs = pairs(lambda g, z, s, c: (g, z ^ 1, s, c))
    core_pairs = pairs(lambda g, z, s, c: (g, z, s, 1 - c))
    jump_pairs, home_jump_pairs = pairs(jumped), pairs(jumped, is_home)

    def cross(a):
        return lax.ppermute(a, AXES, cross_pairs)

    def step(a):
        return lax.ppermute(a, AXES, step_pairs)

    def swap(a):
        return lax.ppermute(a, AXES, core_pairs)

    def home_jump(a):
        return lax.ppermute(a, AXES, home_jump_pairs)

    def jump(a):
        return lax.ppermute(a, AXES, jump_pairs)

    def shards(expected_cot, value_next, transition, section):
        df = factor_of(section)
        z, s, c = lax.axis_index("markov"), lax.axis_index("storage"), lax.axis_index("sub")
        home = z // 2 == s
        mine = z % 2 == c
        half = expected_cot.shape[1] // 2
        quarter = half // 2

        def columns(array, start, stop):
            return array[:, start * quarter : stop * quarter]

        def together(arrays, *gates):
            return lax.optimization_barrier(tuple(arrays) + gates)[: len(arrays)]

        e = [columns(expected_cot, i, i + 1) for i in range(4)]
        v = [columns(value_next, i, i + 1) for i in range(4)]
        x1 = cross(jnp.where(home, v[0], e[0]))
        height = e[3].shape[0]
        rows = height * 5 // 8
        j0 = home_jump(e[3][:rows])
        t_other = swap(transition)
        e2 = after(e[2], x1, j0)
        j1 = jump(jnp.where(home, x1, e2))
        t_near, t_next = jnp.where(mine, transition, t_other), jnp.where(mine, t_other, transition)

        def adjoint_of(near, far):
            return tdot(t_near, near) + tdot(t_next, far)

        v1, e1 = together((v[1], e[1]), x1, t_near)
        x2 = cross(jnp.concatenate([jnp.where(home, v1, e1), v[2]], 1))
        x2, v_across2 = columns(x2, 0, 1), columns(x2, 1, 2)
        near, far = together((e[3][:rows], j0), x1)
        a3_top = jnp.where(home, near, far)
        a3_top_next = step(a3_top)
        second = jnp.where(home, x2, e[3])
        j2 = jump(second)
        near, far = together((j1, v[0]), second)
        third_cross = jnp.where(home, near, far)
        x3 = cross(jnp.concatenate([third_cross, v[3]], 1))
        x3, v_across3 = columns(x3, 0, 1), columns(x3, 1, 2)
        near, far = together((x1, j1), third_cross, a3_top_next)
        b0 = jnp.where(home, near, far)
        b0_next = step(b0)
        third = jnp.where(home, e[0], x3)
        j3 = jump(third)
        sum0 = adjoint_of(b0, b0_next)
        near, far = together((j2, v[1]), third)
        x4 = cross(jnp.where(home, near, far))
        near, far = together((x2, j2), sum0, third)
        b1 = jnp.where(home, near, far)
        b1_next = step(b1)
        part0 = cross(after(sum0, x4))
        fourth = jnp.where(home, e[1], x4)
        j4 = jump(fourth)
        sum1 = adjoint_of(b1, b1_next)
        part1 = cross(after(sum1, part0))
        near, both, far = together((e[0], j3, x3), sum1, fourth)
        a0b2 = jnp.where(home, jnp.concatenate([near, both], 1), jnp.concatenate([both, far], 1))
        a0b2_next = step(a0b2)
        sum2 = adjoint_of(columns(a0b2, 1, 2), columns(a0b2_next, 1, 2))
        part2 = cross(after(sum2, part1))
        rest = jnp.concatenate([e[2], e[3][rows:]], 0)
        j5 = home_jump(after(rest, j3))
        near, both, far = together((e[1], j4, x4), sum2, part0)
        a1b3 = jnp.where(home, jnp.concatenate([near, both], 1), jnp.concatenate([both, far], 1))
        a1b3_next = step(a1b3)
        v_other = swap(after(value_next, sum1))
        sum3 = adjoint_of(columns(a1b3, 1, 2), columns(a1b3_next, 1, 2))
        part3 = cross(after(sum3, part2))

        def own_and_swapped(near, far):
            return jnp.where(mine, near, far), swap(jnp.where(mine, far, near))

        parts = together((x1, x2, x3, x4, v_across2, v_across3), sum1)
        v_across = jnp.concatenate(
            [jnp.where(home, parts[2], parts[0]), jnp.where(home, parts[3], parts[1]), parts[4], parts[5]], 1
        )
        v_across_other = swap(v_across)
        near, far = together((rest, j5), a1b3_next, part1)
        a_rest = jnp.where(home, near, far)
        a_rest_next = step(a_rest)
        b0, b0_next, b1, b1_next, a0b2, a0b2_next = together(
            (b0, b0_next, b1, b1_next, a0b2, a0b2_next), a1b3_next, sum3, part2, a_rest
        )
        a0, a0_next = columns(a0b2, 0, 1), columns(a0b2_next, 0, 1)
        a1, a1_next = columns(a1b3, 0, 1), columns(a1b3_next, 0, 1)
        b_own, b_swapped = own_and_swapped(
            jnp.concatenate([b0, b1, columns(a0b2, 1, 2), columns(a1b3, 1, 2)], 1),
            jnp.concatenate([b0_next, b1_next, columns(a0b2_next, 1, 2), columns(a1b3_next, 1, 2)], 1),
        )
        a01_own, a01_swapped = own_and_swapped(
            jnp.concatenate([a0, a1], 1), jnp.concatenate([a0_next, a1_next], 1)
        )
        grad = dott(
            jnp.concatenate([b_own, b_swapped], 1), jnp.concatenate([v_across, v_across_other], 1)
        ) + dott(
            jnp.concatenate([a01_own, a01_swapped], 1),
            jnp.concatenate([columns(value_next, 0, 2), columns(v_other, 0, 2)], 1),
        )
        own01 = adjoint_of(jnp.concatenate([a0, a1], 1), jnp.concatenate([a0_next, a1_next], 1))
        near, far, near_top, far_top = together((a_rest, a_rest_next, a3_top, a3_top_next), grad, own01)

        def two_quarters(rest, top):
            return jnp.concatenate([rest[:height], jnp.concatenate([top, rest[height:]], 0)], 1)

        near, far = two_quarters(near, near_top), two_quarters(far, far_top)
        a23_own, a23_swapped = own_and_swapped(near, far)
        grad = df * (grad + dott(
            jnp.concatenate([a23_own, a23_swapped], 1),
            jnp.concatenate([columns(value_next, 2, 4), columns(v_other, 2, 4)], 1),
        ))
        own23 = adjoint_of(near, far)
        own23, part3, grad = together((own23, part3, grad))
        adjoint = df * (
            jnp.concatenate([own01, own23], 1) + jnp.concatenate([part0, part1, part2, part3], 1)
        )
        return adjoint, grad

    return shards


def solution(mesh):
    sizes = tuple(mesh.shape[a] for a in AXES)
    shards = two_side_shards(sizes) if sizes[1:] == (4, 2, 2) else plain_shards
    return jax.shard_map(
        shards,
        mesh=mesh,
        in_specs=(
            P(("groups", "markov"), ("storage", "sub")),
            P(("groups", "markov"), ("storage", "sub")),
            P(("groups", "storage", "sub"), "markov"),
            P("groups"),
        ),
        out_specs=(
            P(("groups", "markov"), ("storage", "sub")),
            P(("groups", "storage", "sub"), "markov"),
        ),
        check_vma=False,
    )
```
